32 devices in a mesh: segment: 4 (over z), row: 2 (over x), col: 4 (over y, core).
Axes of the slice: x: 2, y: 2, z: 4, core: 2. Of those that a mesh axis runs over, the one named last changes fastest.
Arguments:
- saved_inputs: bfloat16 [4, 1, 32, 64, 256], P('segment', None, 'row', 'col'), may hold values from -6 to 6
- out_grad: bfloat16 [1, 32, 64, 256], P(None, 'row', 'col'), may hold values from -6 to 6
- tissue: int32 [1, 2, 4], P(None, 'row', 'col'), may hold values 0 or 1
- conv_taps: float32 [4, 7, 7, 256], P('segment'), may hold values from -0.875 to 0.875
- conv_bias: float32 [4, 256], P('segment'), may hold values from -3 to 3
- norm_gain: float32 [4, 256], P('segment'), may hold values from 0.1 to 1.9
- norm_bias: float32 [4, 256], P('segment'), may hold values from -3 to 3
- w_in: bfloat16 [4, 256, 1024], P('segment'), may hold values from -0.375 to 0.375
- b_in: float32 [4, 1024], P('segment'), may hold values from -3 to 3
- w_out: bfloat16 [4, 1024, 256], P('segment'), may hold values from -0.1875 to 0.1875
- layer_scale: float32 [4, 256], P('segment'), may hold values from 0.3 to 1.5
Outputs:
- section_grads: bfloat16 [4, 1, 32, 64, 256], P('segment', None, 'row', 'col')
- grad_w_in: float32 [4, 256, 1024], P('segment', 'col')
- grad_w_out: float32 [4, 1024, 256], P('segment', 'col')
- grad_taps: float32 [4, 7, 7, 256], P('segment')
The draws below stay inside these ranges and needn't reach their ends.
Inputs may be any that keep to these rules, and one draw needn't show every extreme that they name: 1 marks a tile that holds tissue, 0 an empty one.
All inputs are finite; a program needn't handle non-finite values. No bound on the sum of `tissue` on one device may be relied on, other than what follows from the above.
Results may differ from the reference program's by a relative error of at most 0.013.
Values may be sent and summed in bfloat16 or wider, within the bound.
No kernel may reach another device: no remote copies, remote signals or barrier semaphores. Data moves between devices by JAX's collectives and lax.ppermute only.
A program may use at most 128 MiB of HBM per device.

```python
import math
import jax
import jax.numpy as jnp
from jax import lax

C = 256
HID = 1024
KSIZE = 7
TILE = 16
CROPS = 1
SECTIONS = 4
GR = 2
GC = 4
NH = 32
NW = 64


def place_ends(result, rng, least, top_value):
    place = [jax.random.randint(jax.random.fold_in(rng, axis), (), 0, length) for axis, length in enumerate(result.shape)]
    longest = result.shape.index(max(result.shape))
    beside = place[:longest] + [(place[longest] + 1) % result.shape[longest]] + place[longest + 1:]
    return result.at[tuple(place)].set(least).at[tuple(beside)].set(top_value)


def block_scale(stream_key, dims, cuts, smallest, largest):
    factor_of, own = 1.0, jax.random.fold_in(stream_key, 6)
    for axis_at, parts in cuts:
        heights = jnp.exp(jax.random.uniform(jax.random.fold_in(own, axis_at), (parts,), jnp.float32, smallest / len(cuts), largest / len(cuts)))
        factor_of = factor_of * jnp.repeat(heights, dims[axis_at] // parts).reshape([-1 if axis == axis_at else 1 for axis in range(len(dims))])
    return factor_of


def bell_draw(own_key, extent, scale, most, shards=(), dtype=jnp.bfloat16):
    array = jax.random.normal(own_key, extent, jnp.float32) * scale
    if len(shards) > 0:
        array = block_scale(own_key, extent, shards, -0.22, 0.18) * array
    return jnp.clip(array, min=-most, max=most).astype(dtype)


def setup_inputs(seed: int = 0) -> dict:
    streams_of = jax.random.split(jax.random.key(seed), 12)
    return {
        "saved_inputs": bell_draw(streams_of[0], (SECTIONS, CROPS, NH, NW, C), 1.0, 6.0, ((0, 4), (2, 2), (3, 4))),
        "out_grad": bell_draw(streams_of[1], (CROPS, NH, NW, C), 1.0, 6.0, ((1, 2), (2, 4))),
        "tissue": place_ends((jax.random.randint(streams_of[2], (CROPS, GR, GC), 0, 2) < 1).astype(jnp.int32), jax.random.fold_in(streams_of[2], 1), 0, 1),
        "conv_taps": bell_draw(streams_of[3], (SECTIONS, KSIZE, KSIZE, C), (KSIZE * KSIZE) ** -0.5, 0.875, ((0, 4),), jnp.float32),
        "conv_bias": bell_draw(streams_of[4], (SECTIONS, C), 0.5, 3.0, ((0, 4),), jnp.float32),
        "norm_gain": jnp.clip(1.0 + 0.18 * jax.random.normal(streams_of[5], (SECTIONS, C), jnp.float32), 0.1, 1.9),
        "norm_bias": bell_draw(streams_of[6], (SECTIONS, C), 0.5, 3.0, ((0, 4),), jnp.float32),
        "w_in": bell_draw(streams_of[7], (SECTIONS, C, HID), C ** -0.5, 0.375, ((0, 4),)),
        "b_in": bell_draw(streams_of[8], (SECTIONS, HID), 0.5, 3.0, ((0, 4),), jnp.float32),
        "w_out": bell_draw(streams_of[9], (SECTIONS, HID, C), HID ** -0.5, 0.1875, ((0, 4),)),
        "layer_scale": jnp.clip(jnp.exp(math.log(1.5) - 1.60943787 * jax.random.uniform(streams_of[10], (SECTIONS, C), jnp.float32) ** block_scale(streams_of[10], (SECTIONS, C), ((0, 4),), -0.2, 0.2)), 0.3, 1.5),
    }


epsilon = 1e-06

def depthwise(padded, conv_taps, height, across):
    side = conv_taps.shape[0]
    total = jnp.zeros((height, across, padded.shape[-1]), jnp.float32)
    for shift_r in range(side):
        for shift_c in range(side):
            total = total + conv_taps[shift_r, shift_c] * padded[shift_r:shift_r + height, shift_c:shift_c + across].astype(jnp.float32)
    return total

def transposed(padded_grad, conv_taps, height, across):
    side = conv_taps.shape[0]
    margin = side // 2
    total = jnp.zeros((height, across, padded_grad.shape[-1]), jnp.float32)
    for shift_r in range(side):
        for shift_c in range(side):
            start_r = 2 * margin - shift_r
            start_c = 2 * margin - shift_c
            total = total + conv_taps[shift_r, shift_c] * padded_grad[start_r:start_r + height, start_c:start_c + across].astype(jnp.float32)
    return total

def kernel_grad(padded, grad, height, across):
    side = KSIZE
    grad_wide = grad.astype(jnp.float32)
    pieces = []
    for shift_r in range(side):
        for shift_c in range(side):
            window = padded[shift_r:shift_r + height, shift_c:shift_c + across].astype(jnp.float32)
            pieces.append(lax.optimization_barrier(jnp.sum(window * grad_wide, axis=(0, 1))))
    return jnp.stack(pieces).reshape(side, side, -1)

def pixel_grad(conv_out, upstream, gate, norm_gain, norm_bias, w_in, b_in, w_out, layer_scale):
    average = lax.optimization_barrier(jnp.mean(conv_out, axis=-1, keepdims=True))
    centred = conv_out - average
    spread = lax.optimization_barrier(jnp.mean(centred * centred, axis=-1, keepdims=True))
    inv_std = lax.rsqrt(spread + epsilon)
    standard = centred * inv_std
    normed = (standard * norm_gain + norm_bias).astype(jnp.bfloat16)
    pre_gate = jnp.dot(normed, w_in, preferred_element_type=jnp.float32) + b_in
    gated, gelu_back = jax.vjp(jax.nn.gelu, pre_gate)
    hidden = gated.astype(jnp.bfloat16)
    branch_grad = (gate * layer_scale * upstream.astype(jnp.float32)).astype(jnp.bfloat16)
    grad_out = jnp.dot(hidden.T, branch_grad, preferred_element_type=jnp.float32)
    hidden_grad = jnp.dot(branch_grad, w_out.T, preferred_element_type=jnp.float32)
    pre_grad = gelu_back(hidden_grad)[0].astype(jnp.bfloat16)
    grad_in = jnp.dot(normed.T, pre_grad, preferred_element_type=jnp.float32)
    norm_grad = jnp.dot(pre_grad, w_in.T, preferred_element_type=jnp.float32) * norm_gain
    conv_grad = inv_std * (norm_grad - lax.optimization_barrier(jnp.mean(norm_grad, axis=-1, keepdims=True)) - standard * lax.optimization_barrier(jnp.mean(norm_grad * standard, axis=-1, keepdims=True)))
    return (conv_grad.astype(jnp.bfloat16), grad_in, grad_out)

def reference(saved_inputs, out_grad, tissue, conv_taps, conv_bias, norm_gain, norm_bias, w_in, b_in, w_out, layer_scale):
    margin = KSIZE // 2
    norm_scale = 1.0 / math.sqrt(CROPS * NH * NW)
    upstream_all = out_grad
    section_list = [None] * SECTIONS
    grad_in_list = [None] * SECTIONS
    grad_out_list = [None] * SECTIONS
    grad_taps_list = [None] * SECTIONS
    for section in range(SECTIONS - 1, -1, -1):
        sum_in = jnp.zeros((C, HID), jnp.float32)
        sum_out = jnp.zeros((HID, C), jnp.float32)
        sum_taps = jnp.zeros((KSIZE, KSIZE, C), jnp.float32)
        crop_grads = []
        for crop in range(CROPS):
            saved = saved_inputs[section, crop]
            upstream = upstream_all[crop]
            padded = jnp.pad(saved, ((margin, margin), (margin, margin), (0, 0)))
            conv_out = depthwise(padded, conv_taps[section], NH, NW) + conv_bias[section]
            tile_marks = tissue[crop].astype(jnp.float32)
            pixel_mask = jnp.broadcast_to(tile_marks[:, None, :, None], (GR, TILE, GC, TILE)).reshape(NH, NW)
            conv_grad, grad_in, grad_out = pixel_grad(conv_out.reshape(-1, C), upstream.reshape(-1, C), pixel_mask.reshape(-1, 1), norm_gain[section], norm_bias[section], w_in[section], b_in[section], w_out[section], layer_scale[section])
            conv_grad = conv_grad.reshape(NH, NW, C)
            sum_in = sum_in + grad_in
            sum_out = sum_out + grad_out
            sum_taps = sum_taps + kernel_grad(padded, conv_grad, NH, NW)
            padded_grad = jnp.pad(conv_grad, ((margin, margin), (margin, margin), (0, 0)))
            input_grad = (upstream.astype(jnp.float32) + transposed(padded_grad, conv_taps[section], NH, NW)).astype(jnp.bfloat16)
            crop_grads.append(input_grad)
        upstream_all = jnp.stack(crop_grads)
        section_list[section] = upstream_all
        grad_in_list[section] = sum_in * norm_scale
        grad_out_list[section] = sum_out * norm_scale
        grad_taps_list[section] = sum_taps * norm_scale
    return (jnp.stack(section_list), jnp.stack(grad_in_list), jnp.stack(grad_out_list), jnp.stack(grad_taps_list))
```

```python
import functools
import math

import jax
import jax.numpy as jnp
from jax import lax
from jax.experimental import pallas as pl
from jax.experimental.pallas import tpu as pltpu
from jax.sharding import PartitionSpec as P

epsilon = 1e-06
PAD = 8
LANES = 128
VMEM_BYTES = 48 * 1024 * 1024
LINE = ("segment", "row", "col")

f32 = jnp.float32
bf16 = jnp.bfloat16


class Plan:
    def __init__(self, segments, rows, cols, height, across, channels, hidden, side):
        self.segments, self.rows, self.cols = segments, rows, cols
        self.height, self.across = height, across
        self.channels, self.hidden, self.side = channels, hidden, side
        self.margin = side // 2
        self.width = across // rows
        self.full = height * rows
        self.padded = self.width + 2 * self.margin
        self.cells = self.width * self.full
        self.part = min(256, hidden)

    def main_size(self):
        sizes = []
        for r in range(self.rows):
            low = max(0, r * self.width - self.margin)
            high = min(self.across, (r + 1) * self.width + self.margin)
            sizes.append(high - low)
        return max(sizes)

    def main_start(self, r):
        return jnp.clip(r * self.width - self.margin, 0, self.across - self.main_size())

    def needs_left(self, r):
        return r * self.width < self.margin

    def needs_right(self, r):
        return (r + 1) * self.width + self.margin > self.across

    def sides(self):
        left = [r for r in range(self.rows) if self.needs_left(r)]
        right = [r for r in range(self.rows) if self.needs_right(r)]
        if set(left) & set(right):
            return [(left, []), ([], right)]
        return [(left, right)]

    def distances(self):
        out = []
        distance = 1
        while (distance - 1) * self.width < self.margin:
            out.append((distance, min(self.width, self.margin - (distance - 1) * self.width)))
            distance += 1
        return out

    def index(self, s, r, c):
        return (s * self.rows + r) * self.cols + c

    def strip(self, s, t):
        return self.index(s, t % self.rows, t // self.rows)

    def own(self, column):
        return self.margin <= column < self.margin + self.width


def vmem():
    return pl.BlockSpec(memory_space=pltpu.VMEM)


def smem():
    return pl.BlockSpec(memory_space=pltpu.SMEM)


def shape(dims, dtype):
    return jax.ShapeDtypeStruct(tuple(dims), dtype)


def call(kernel, name, operands, outs, scratch, flops):
    moved = sum(math.prod(o.shape) * o.dtype.itemsize for o in list(operands) + list(outs))
    return pl.pallas_call(
        kernel,
        out_shape=outs,
        in_specs=[vmem()] * len(operands),
        out_specs=[vmem()] * len(outs),
        scratch_shapes=scratch,
        compiler_params=pltpu.CompilerParams(vmem_limit_bytes=VMEM_BYTES),
        cost_estimate=pl.CostEstimate(flops=flops, bytes_accessed=moved, transcendentals=0),
        name=name,
    )(*operands)


def pack_kernel(plan, params, tissue_ref, x_hbm, g_hbm, *refs):
    rows, across, height = plan.rows, plan.across, plan.height
    count = rows * (1 + len(plan.sides()))
    sources, refs = refs[:params], refs[params:]
    outs, refs = refs[:count], refs[count:]
    targets, (x_ref, g_ref, xt, gt, sems) = refs[:params], refs[params:]
    moves = [
        pltpu.make_async_copy(source, target, sems.at[k])
        for k, (source, target) in enumerate(zip((x_hbm, g_hbm, *sources), (x_ref, g_ref, *targets)))
    ]
    for move in moves:
        move.start()
    tiles_r, tiles_c = tissue_ref.shape
    side_r, side_c = height // tiles_r, across // tiles_c
    me = lax.axis_index("row")
    row_at = lax.broadcasted_iota(jnp.int32, (height, plan.channels), 0)
    lane_at = lax.broadcasted_iota(jnp.int32, (height, plan.channels), 1)

    def slot(start):
        col_at = lane_at + start
        total = jnp.zeros((height, plan.channels), f32)
        for a in range(tiles_r):
            in_row = (row_at >= a * side_r) & (row_at < (a + 1) * side_r)
            for b in range(tiles_c):
                inside = in_row & (col_at >= b * side_c) & (col_at < (b + 1) * side_c)
                total = jnp.where(inside, tissue_ref[a, b].astype(f32), total)
        return total.astype(bf16)

    moves[0].wait()
    xt[...] = jnp.swapaxes(x_ref[...].astype(f32), 0, 1).astype(bf16)
    moves[1].wait()
    gt[...] = jnp.swapaxes(g_ref[...].astype(f32), 0, 1).astype(bf16)
    nx, m, w = plan.main_size(), plan.margin, plan.width
    for dr in range(rows):
        target = lax.rem(me - dr + rows, rows)
        out = outs[dr]
        out[0:nx] = xt[pl.ds(plan.main_start(target), nx)]
        out[nx : nx + w] = gt[pl.ds(target * w, w)]
        out[nx + w] = slot(target * w)
    for k, (left, right) in enumerate(plan.sides()):
        for dr in range(rows):
            target = lax.rem(me - dr + rows, rows)
            is_left = functools.reduce(jnp.logical_or, [target == r for r in left], jnp.bool_(False))
            outs[rows * (1 + k) + dr][...] = xt[pl.ds(jnp.where(is_left, across - m, 0), m)]
    for move in moves[2:]:
        move.wait()


def pack(plan, tissue, x, g, params):
    rows, h, c = plan.rows, plan.height, plan.channels
    outs = [shape((plan.main_size() + plan.width + 1, h, c), bf16)] * rows
    outs += [shape((plan.margin, h, c), bf16)] * (rows * len(plan.sides()))
    outs += [shape(a.shape, a.dtype) for a in params]
    tile = pltpu.VMEM((h, plan.across, c), bf16)
    turned = pltpu.VMEM((plan.across, h, c), bf16)
    count = len(params)
    out = pl.pallas_call(
        functools.partial(pack_kernel, plan, count),
        out_shape=outs,
        in_specs=[smem()] + [pl.BlockSpec(memory_space=pltpu.HBM)] * (2 + count),
        out_specs=[vmem()] * len(outs),
        scratch_shapes=[tile, tile, turned, turned, pltpu.SemaphoreType.DMA((2 + count,))],
        compiler_params=pltpu.CompilerParams(vmem_limit_bytes=VMEM_BYTES),
        cost_estimate=pl.CostEstimate(flops=1000, bytes_accessed=4 << 20, transcendentals=0),
        name="pack",
    )(tissue, x, g, *params)
    return out[:-count], out[-count:]


def exchange(plan, pieces):
    rows, cols = plan.rows, plan.cols
    mains, sides = [pieces[0]], []
    for k, (left, right) in enumerate(plan.sides()):
        for dr in range(rows):
            pairs = []
            for s in range(plan.segments):
                for r in range(rows):
                    for c in range(cols):
                        step = (-1 if r in left else 0) + (1 if r in right else 0)
                        if step != 0 and 0 <= c + step < cols:
                            source = plan.index(s, (r + dr) % rows, c + step)
                            pairs.append((source, plan.index(s, r, c)))
            sides.append(lax.ppermute(pieces[rows * (1 + k) + dr], LINE, pairs))
    for dr in range(1, rows):
        pairs = []
        for s in range(plan.segments):
            for r in range(rows):
                for c in range(cols):
                    pairs.append((plan.index(s, (r + dr) % rows, c), plan.index(s, r, c)))
        mains.append(lax.ppermute(pieces[dr], LINE, pairs))
    return mains + sides


def conv_block(plan, load, row_start, half, taps_ref, flip, keep):
    side = plan.side
    lanes = pl.ds(half * LANES, LANES)
    totals = [None] * plan.width
    for i in range(side):
        rows_at = pl.ds(row_start + (side - 1 - i if flip else i), 8)
        window = [load(k, rows_at, lanes) if keep(k) else None for k in range(plan.padded)]
        for j in range(side):
            tap = taps_ref[i, pl.ds(j, 1), lanes]
            move = side - 1 - j if flip else j
            for q in range(plan.width):
                if window[q + move] is not None:
                    term = tap * window[q + move]
                    totals[q] = term if totals[q] is None else totals[q] + term
    return [jnp.zeros((8, LANES), f32) if t is None else t for t in totals]


def clear_rims(ref, full):
    zeros = jnp.zeros((ref.shape[0], PAD, ref.shape[2]), ref.dtype)
    ref[:, 0:PAD, :] = zeros
    ref[:, PAD + full : PAD + full + PAD, :] = zeros


def blocks(plan):
    return [(half, block) for half in range(plan.channels // LANES) for block in range(plan.full // 8)]


def forward_kernel(plan, *refs):
    rows, full, h = plan.rows, plan.full, plan.height
    pieces = refs[: rows * (1 + len(plan.sides()))]
    refs = refs[len(pieces) :]
    (taps_ref, conv_bias_ref, gain_ref, bias_ref, w_in_ref, b_in_ref) = refs[:6]
    (og_ref, xw_ref, mask_ref, standard_ref, inv_ref, gate_ref, hidden_ref, normed_ref) = refs[6:14]
    wide_x, conv_ref, pre_ref = refs[14:]
    me = lax.axis_index("row")
    m, w, nx = plan.margin, plan.width, plan.main_size()

    clear_rims(wide_x, full)
    for dr in range(rows):
        piece = pieces[dr]
        top = pl.multiple_of(lax.rem(me + dr, rows) * h, h)
        wide_x[pl.ds(m + plan.main_start(me), nx), pl.ds(PAD + top, h), :] = piece[0:nx].astype(f32)
        og_ref[:, pl.ds(top, h), :] = piece[nx : nx + w]
        marks = piece[nx + w].astype(f32)
        for l in range(w):
            at = pl.ds(pl.multiple_of(l * full + top, h), h)
            mask_ref[at, :] = jnp.broadcast_to(marks[:, l : l + 1], (h, LANES))
    for k, (left, right) in enumerate(plan.sides()):
        is_left = functools.reduce(jnp.logical_or, [me == r for r in left], jnp.bool_(False))
        for dr in range(rows):
            top = pl.multiple_of(lax.rem(me + dr, rows) * h, h)
            start = jnp.where(is_left, 0, m + plan.across)
            piece = pieces[rows * (1 + k) + dr]
            wide_x[pl.ds(start, m), pl.ds(PAD + top, h), :] = piece[...].astype(f32)

    base = me * w
    xw_ref[...] = wide_x[pl.ds(base, plan.padded)]

    def load(column, rows_at, lanes):
        return wide_x[base + column, rows_at, lanes]

    for half, block in blocks(plan):
        lanes = pl.ds(half * LANES, LANES)
        sums = conv_block(plan, load, PAD - m + 8 * block, half, taps_ref, False, lambda k: True)
        for q in range(w):
            conv_ref[pl.ds(q * full + 8 * block, 8), lanes] = sums[q] + conv_bias_ref[:, lanes]

    for col in range(w):
        rows_at = pl.ds(col * full, full)
        conv_out = conv_ref[rows_at, :]
        average = jnp.mean(conv_out, axis=-1, keepdims=True)
        centred = conv_out - average
        spread = jnp.mean(centred * centred, axis=-1, keepdims=True)
        inv_std = lax.rsqrt(spread + epsilon)
        standard = centred * inv_std
        standard_ref[rows_at, :] = standard
        inv_ref[rows_at, :] = jnp.broadcast_to(inv_std, (full, LANES))
        normed_ref[rows_at, :] = (standard * gain_ref[...] + bias_ref[...]).astype(bf16)

    c1 = math.sqrt(2.0 / math.pi)
    c2 = c1 * 0.044715
    for n in range(plan.hidden // plan.part):
        at = pl.ds(n * plan.part, plan.part)
        pre_ref[n % 2] = (
            jnp.dot(normed_ref[...], w_in_ref[:, at], preferred_element_type=f32) + b_in_ref[:, at]
        )
        for col in range(w):
            rows_at = pl.ds(col * full, full)
            pre = pre_ref[n % 2, rows_at, :]
            square = pre * pre
            half_one = 0.5 + 0.5 * jnp.tanh(pre * (c1 + c2 * square))
            gated = pre * half_one
            slope = half_one + gated * (1.0 - half_one) * (2.0 * c1 + 6.0 * c2 * square)
            gate_ref[rows_at, at] = slope.astype(bf16)
            hidden_ref[rows_at, at] = gated.astype(bf16)


def forward(plan, pieces, taps, conv_bias, gain, bias, w_in, b_in):
    c, full, cells = plan.channels, plan.full, plan.cells
    outs = [
        shape((plan.width, full, c), bf16),
        shape((plan.padded, full + 2 * PAD, c), f32),
        shape((cells, LANES), f32),
        shape((cells, c), f32),
        shape((cells, LANES), f32),
        shape((cells, plan.hidden), bf16),
        shape((cells, plan.hidden), bf16),
        shape((cells, c), bf16),
    ]
    scratch = [
        pltpu.VMEM((plan.across + 2 * plan.margin, full + 2 * PAD, c), f32),
        pltpu.VMEM((cells, c), f32),
        pltpu.VMEM((2, cells, plan.part), f32),
    ]
    return call(
        functools.partial(forward_kernel, plan),
        "forward",
        [*pieces, taps, conv_bias, gain, bias, w_in, b_in],
        outs,
        scratch,
        2 * cells * c * plan.hidden,
    )


def across_lanes(value, channels):
    return jnp.concatenate([value] * (channels // LANES), axis=-1)


def fill_edges(plan, edge_ref, edges):
    clear_rims(edge_ref, plan.full)
    m, w = plan.margin, plan.width
    for k, (distance, count) in enumerate(plan.distances()):
        for start, piece in (
            (m - (distance - 1) * w - count, edges[2 * k]),
            (m + distance * w, edges[2 * k + 1]),
        ):
            edge_ref[pl.ds(start, count), PAD : PAD + plan.full, :] = piece[...].astype(f32)


def edge_sums(plan, edge_ref, taps_ref, half, block):
    def load(column, rows_at, lanes):
        return edge_ref[column, rows_at, lanes]

    start = PAD - plan.margin + 8 * block
    return conv_block(plan, load, start, half, taps_ref, True, lambda k: not plan.own(k))


def own_sums(plan, cg_ref, taps_ref, half, block):
    def load(column, rows_at, lanes):
        return cg_ref[column - plan.margin, rows_at, lanes]

    start = PAD - plan.margin + 8 * block
    return conv_block(plan, load, start, half, taps_ref, True, plan.own)


def load_upstream(plan, g_ref, og_ref, received, edge_ref):
    if received is None:
        g_ref[...] = og_ref[...]
        return
    taps_ref, main_ref, edges = received[0], received[1], received[2:]
    last = lax.axis_index("segment") == plan.segments - 1
    fill_edges(plan, edge_ref, edges)
    for half, block in blocks(plan):
        if block % 2:
            continue
        lanes = pl.ds(half * LANES, LANES)
        rows_at = pl.ds(8 * block, 16)
        parts = [edge_sums(plan, edge_ref, taps_ref, half, block + k) for k in range(2)]
        for q in range(plan.width):
            rest = jnp.concatenate([part[q] for part in parts], axis=0)
            value = (main_ref[q, rows_at, lanes].astype(f32) + rest).astype(bf16)
            g_ref[q, rows_at, lanes] = jnp.where(last, og_ref[q, rows_at, lanes], value)


def norm_back(plan, norm_grad_ref, gain_ref, standard_ref, inv_ref, cg_ref):
    full = plan.full
    clear_rims(cg_ref, full)
    for col in range(plan.width):
        rows_at = pl.ds(col * full, full)
        norm_grad = norm_grad_ref[rows_at, :] * gain_ref[...]
        standard = standard_ref[rows_at, :]
        inv_std = across_lanes(inv_ref[rows_at, :], plan.channels)
        grad = inv_std * (
            norm_grad
            - jnp.mean(norm_grad, axis=-1, keepdims=True)
            - standard * jnp.mean(norm_grad * standard, axis=-1, keepdims=True)
        )
        cg_ref[col, PAD : PAD + full, :] = grad.astype(bf16).astype(f32)


def contract_last(a, b):
    return lax.dot_general(a, b, (((1,), (1,)), ((), ())), preferred_element_type=f32)


def branch(plan, g_ref, scale_ref, mask_ref, bg_ref):
    full = plan.full
    for col in range(plan.width):
        rows_at = pl.ds(col * full, full)
        mask = across_lanes(mask_ref[rows_at, :], plan.channels)
        bg_ref[rows_at, :] = (mask * scale_ref[...] * g_ref[col].astype(f32)).astype(bf16)


def put_edges(plan, cg_ref, outs):
    rows_at = pl.ds(PAD, plan.full)
    for k, (distance, count) in enumerate(plan.distances()):
        outs[2 * k][...] = cg_ref[pl.ds(plan.width - count, count), rows_at, :].astype(bf16)
        outs[2 * k + 1][...] = cg_ref[pl.ds(0, count), rows_at, :].astype(bf16)


def edge_shapes(plan):
    return [
        shape((count, plan.full, plan.channels), bf16) for _, count in plan.distances() for _ in range(2)
    ]


def send_edges(plan, edges, step):
    strips = plan.rows * plan.cols
    received = []
    for k, (distance, _) in enumerate(plan.distances()):
        for way, piece in ((distance, edges[2 * k]), (-distance, edges[2 * k + 1])):
            pairs = [
                (plan.strip(s, t), plan.strip(s + step, t + way))
                for s in range(plan.segments)
                for t in range(strips)
                if 0 <= t + way < strips and 0 <= s + step < plan.segments
            ]
            received.append(lax.ppermute(piece, LINE, pairs))
    return received


def to_segment_below(plan, value):
    return lax.ppermute(value, "segment", [(s, s - 1) for s in range(1, plan.segments)])


def step_kernel(plan, n_received, og_ref, *refs):
    received = refs[:n_received] or None
    refs = refs[n_received:]
    (scale_ref, gain_ref, w_in_ref, w_out_ref, gate_ref, mask_ref, standard_ref, inv_ref, taps_ref) = refs[:9]
    count = 2 * len(plan.distances())
    new_ref, edges = refs[9], refs[10 : 10 + count]
    g_ref, bg_ref, ng_ref, cg_ref, edge_ref = refs[10 + count :]
    load_upstream(plan, g_ref, og_ref, received, edge_ref)
    branch(plan, g_ref, scale_ref, mask_ref, bg_ref)
    for n in range(plan.hidden // plan.part):
        at = pl.ds(n * plan.part, plan.part)
        hidden_grad = contract_last(bg_ref[...], w_out_ref[at, :])
        pre_grad = (hidden_grad * gate_ref[:, at].astype(f32)).astype(bf16)
        term = contract_last(pre_grad, w_in_ref[:, at])
        ng_ref[...] = term if n == 0 else ng_ref[...] + term
    norm_back(plan, ng_ref, gain_ref, standard_ref, inv_ref, cg_ref)
    put_edges(plan, cg_ref, edges)
    for half, block in blocks(plan):
        if block % 2:
            continue
        lanes = pl.ds(half * LANES, LANES)
        rows_at = pl.ds(8 * block, 16)
        parts = [own_sums(plan, cg_ref, taps_ref, half, block + k) for k in range(2)]
        for q in range(plan.width):
            moved = jnp.concatenate([part[q] for part in parts], axis=0)
            new_ref[q, rows_at, lanes] = (g_ref[q, rows_at, lanes].astype(f32) + moved).astype(bf16)


def backward_step(plan, og, received, params, saved):
    scale, gain, w_in, w_out, taps = params
    standard, inv, gate, mask = saved
    c, full, cells = plan.channels, plan.full, plan.cells
    outs = [shape((plan.width, full, c), bf16), *edge_shapes(plan)]
    scratch = [
        pltpu.VMEM((plan.width, full, c), bf16),
        pltpu.VMEM((cells, c), bf16),
        pltpu.VMEM((cells, c), f32),
        pltpu.VMEM((plan.width, full + 2 * PAD, c), f32),
        pltpu.VMEM((plan.padded, full + 2 * PAD, c), f32),
    ]
    return call(
        functools.partial(step_kernel, plan, len(received)),
        "backward",
        [og, *received, scale, gain, w_in, w_out, gate, mask, standard, inv, taps],
        outs,
        scratch,
        4 * cells * c * plan.hidden,
    )


def turn_kernel(hidden_ref, normed_ref, hidden_t_ref, normed_t_ref):
    hidden_t_ref[...] = hidden_ref[...].astype(f32).T.astype(bf16)
    normed_t_ref[...] = normed_ref[...].astype(f32).T.astype(bf16)


def turn(hidden, normed):
    outs = [shape(hidden.shape[::-1], bf16), shape(normed.shape[::-1], bf16)]
    return call(turn_kernel, "turn", [hidden, normed], outs, [], 1000)


def out_share(plan):
    return plan.hidden // plan.cols


def in_share(plan):
    rows = plan.channels // plan.cols
    return rows, plan.hidden // plan.part * rows


def taps_rows(plan):
    return -(-(plan.side**2) // 16) * 16


def put(halves_ref, bit, share, row, value):
    half = bit if share % 2 == 0 else 1 - bit
    halves_ref[half, share // 2, pl.ds(row, value.shape[0]), :] = value


def out_kernel(plan, n_received, og_ref, *refs):
    received = refs[:n_received] or None
    scale_ref, mask_ref, hidden_t_ref, g_ref, bg_ref, halves_ref, send_ref, edge_ref = refs[n_received:]
    load_upstream(plan, g_ref, og_ref, received, edge_ref)
    branch(plan, g_ref, scale_ref, mask_ref, bg_ref)
    bit = lax.rem(lax.axis_index("col"), 2)
    rows = out_share(plan)
    piece = min(plan.part, rows)
    for n in range(plan.hidden // plan.part):
        at = pl.ds(n * plan.part, plan.part)
        grad_out = jnp.dot(hidden_t_ref[at, :], bg_ref[...], preferred_element_type=f32)
        for start in range(0, plan.part, piece):
            unit = n * plan.part + start
            put(halves_ref, bit, unit // rows, unit % rows, grad_out[start : start + piece])
    for u in range(plan.cols // 2):
        send_ref[pl.ds(u * rows, rows), :] = halves_ref[1, u].astype(bf16)


def out_step(plan, og, received, scale, mask, hidden_t):
    c, full, cells, half = plan.channels, plan.full, plan.cells, plan.cols // 2
    rows = out_share(plan)
    outs = [
        shape((plan.width, full, c), bf16),
        shape((cells, c), bf16),
        shape((2, half, rows, c), f32),
        shape((half * rows, c), bf16),
    ]
    return call(
        functools.partial(out_kernel, plan, len(received)),
        "grad_out",
        [og, *received, scale, mask, hidden_t],
        outs,
        [pltpu.VMEM((plan.padded, full + 2 * PAD, c), f32)],
        2 * cells * c * plan.hidden,
    )


def in_kernel(plan, bg_ref, w_in_ref, w_out_ref, gate_ref, normed_t_ref, ng_ref, halves_ref):
    bit = lax.rem(lax.axis_index("col"), 2)
    rows, _ = in_share(plan)
    for n in range(plan.hidden // plan.part):
        at = pl.ds(n * plan.part, plan.part)
        hidden_grad = contract_last(bg_ref[...], w_out_ref[at, :])
        pre_grad = (hidden_grad * gate_ref[:, at].astype(f32)).astype(bf16)
        term = contract_last(pre_grad, w_in_ref[:, at])
        ng_ref[...] = term if n == 0 else ng_ref[...] + term
        grad_in = jnp.dot(normed_t_ref[...], pre_grad, preferred_element_type=f32)
        for share in range(plan.cols):
            put(halves_ref, bit, share, n * rows, grad_in[share * rows : (share + 1) * rows])


def in_step(plan, bg, w_in, w_out, gate, normed_t):
    c, cells = plan.channels, plan.cells
    outs = [shape((cells, c), f32), shape((2, plan.cols // 2, in_share(plan)[1], c), f32)]
    return call(
        functools.partial(in_kernel, plan),
        "grad_in",
        [bg, w_in, w_out, gate, normed_t],
        outs,
        [],
        6 * cells * c * plan.hidden,
    )


def taps_kernel(plan, ng_ref, halves_ref, gain_ref, standard_ref, inv_ref, xw_ref, cg_ref, send_ref, *edges):
    full, width, side = plan.full, plan.width, plan.side
    _, share_rows = in_share(plan)
    norm_back(plan, ng_ref, gain_ref, standard_ref, inv_ref, cg_ref)
    put_edges(plan, cg_ref, edges)
    count = plan.cols // 2
    for u in range(count):
        send_ref[pl.ds(u * share_rows, share_rows), :] = halves_ref[1, u].astype(bf16)
    rows = []
    for i in range(side):
        pieces = [[] for _ in range(side)]
        for half in range(plan.channels // LANES):
            lanes = pl.ds(half * LANES, LANES)
            totals = [jnp.zeros((8, LANES), f32) for _ in range(side)]
            for block in range(full // 8):
                window = xw_ref[:, pl.ds(PAD - plan.margin + i + 8 * block, 8), lanes]
                grad = cg_ref[:, pl.ds(PAD + 8 * block, 8), lanes]
                for j in range(side):
                    totals[j] = totals[j] + jnp.sum(window[j : j + width] * grad, axis=0)
            for j in range(side):
                pieces[j].append(jnp.sum(totals[j], axis=0, keepdims=True))
        rows += [jnp.concatenate(p, axis=-1) for p in pieces]
    rows.append(jnp.zeros((taps_rows(plan) - side**2, plan.channels), f32))
    at = pl.ds(count * share_rows, taps_rows(plan))
    send_ref[at, :] = jnp.concatenate(rows, axis=0).astype(bf16)


def taps_step(plan, norm_grad, halves, gain, standard, inv, xw):
    c, full = plan.channels, plan.full
    outs = [
        shape((plan.width, full + 2 * PAD, c), f32),
        shape((plan.cols // 2 * in_share(plan)[1] + taps_rows(plan), c), bf16),
        *edge_shapes(plan),
    ]
    return call(
        functools.partial(taps_kernel, plan),
        "grad_taps",
        [norm_grad, halves, gain, standard, inv, xw],
        outs,
        [],
        2 * plan.cells * c * plan.side**2,
    )


def finish_kernel(plan, g_ref, cg_ref, taps_ref, *refs):
    edges, (new_ref, edge_ref) = refs[:-2], refs[-2:]
    fill_edges(plan, edge_ref, edges)
    for half, block in blocks(plan):
        if block % 2:
            continue
        lanes = pl.ds(half * LANES, LANES)
        own = [own_sums(plan, cg_ref, taps_ref, half, block + k) for k in range(2)]
        rest = [edge_sums(plan, edge_ref, taps_ref, half, block + k) for k in range(2)]
        r, at = divmod(8 * block, plan.height)
        for q in range(plan.width):
            moved = jnp.concatenate([own[k][q] + rest[k][q] for k in range(2)], axis=0)
            upstream = g_ref[q, pl.ds(8 * block, 16), lanes].astype(f32)
            new_ref[r, q, pl.ds(at, 16), lanes] = (upstream + moved).astype(bf16)


def finish(plan, upstream, conv_grad, taps, edges):
    c = plan.channels
    return call(
        functools.partial(finish_kernel, plan),
        "finish",
        [upstream, conv_grad, taps, *edges],
        [shape((plan.rows, plan.width, plan.height, c), bf16)],
        [pltpu.VMEM((plan.padded, plan.full + 2 * PAD, c), f32)],
        2 * plan.cells * c * plan.side**2,
    )[0]


def swap(value, axis, bit):
    size = lax.axis_size(axis)
    return lax.ppermute(value, axis, [(i, i ^ bit) for i in range(size)])


def combine_kernel(bit, share_rows, extra, keep_ref, sent_ref, got_ref, send_ref, next_ref):
    count = keep_ref.shape[1]
    mine = lax.rem(lax.axis_index("col") // bit, 2)
    for u in range(count // 2):
        for half in range(2):
            share = 2 * u + (mine if half == 0 else 1 - mine)
            at = pl.ds(pl.multiple_of(share * share_rows, 16), share_rows)
            value = keep_ref[0, share] + got_ref[at, :].astype(f32)
            if half == 0:
                next_ref[0, u] = value
            else:
                send_ref[pl.ds(u * share_rows, share_rows), :] = value.astype(bf16)
    if extra:
        old = pl.ds(count * share_rows, extra)
        new = pl.ds(count // 2 * share_rows, extra)
        send_ref[new, :] = (sent_ref[old, :].astype(f32) + got_ref[old, :].astype(f32)).astype(bf16)


def close_kernel(share_rows, extra, keep_ref, sent_ref, got_ref, out_ref):
    at = pl.ds(0, share_rows)
    out_ref[at, :] = (keep_ref[0, 0] + got_ref[at, :].astype(f32)).astype(bf16)
    if extra:
        rest = pl.ds(share_rows, extra)
        out_ref[rest, :] = (sent_ref[rest, :].astype(f32) + got_ref[rest, :].astype(f32)).astype(bf16)


class Reduction:
    def __init__(self, plan, halves, send, share_rows, extra):
        self.plan, self.share_rows, self.extra = plan, share_rows, extra
        self.keep, self.send, self.bit = halves, send, 1
        if plan.cols > 2:
            self.next_stage()

    def next_stage(self):
        c = self.plan.channels
        got = swap(self.send, "col", self.bit)
        self.bit *= 2
        count = self.keep.shape[1] // 2
        self.send, self.keep = call(
            functools.partial(combine_kernel, self.bit, self.share_rows, self.extra),
            "combine",
            [self.keep, self.send, got],
            [
                shape((count * self.share_rows + self.extra, c), bf16),
                shape((1, count, self.share_rows, c), f32),
            ],
            [],
            1000,
        )

    def terms(self):
        plan = self.plan
        while 2 * self.bit < plan.cols:
            self.next_stage()
        got = swap(self.send, "col", self.bit)
        total = call(
            functools.partial(close_kernel, self.share_rows, self.extra),
            "close",
            [self.keep, self.send, got],
            [shape((self.share_rows + self.extra, plan.channels), bf16)],
            [],
            1000,
        )[0]
        terms = [total]
        bit = 1
        while bit < plan.rows:
            terms = [total, swap(total, "row", bit)]
            bit *= 2
            if bit < plan.rows:
                total = (terms[0].astype(f32) + terms[1].astype(f32)).astype(bf16)
        return terms


def read(refs, scale, start, count):
    return scale * sum(ref[pl.ds(start, count), :].astype(f32) for ref in refs)


def out_result_kernel(plan, scale, *refs):
    refs[-1][...] = read(refs[:-1], scale, 0, out_share(plan))


def in_result_kernel(plan, scale, *refs):
    terms, (in_ref, taps_ref) = refs[:-2], refs[-2:]
    rows, share_rows = in_share(plan)
    for n in range(plan.hidden // plan.part):
        in_ref[:, pl.ds(n * plan.part, plan.part)] = read(terms, scale, n * rows, rows)
    sums = read(terms, scale, share_rows, taps_rows(plan))
    for i in range(plan.side):
        taps_ref[i] = sums[i * plan.side : (i + 1) * plan.side]


def out_result(plan, scale, terms):
    kernel = functools.partial(out_result_kernel, plan, scale)
    return call(kernel, "out_result", terms, [shape((out_share(plan), plan.channels), f32)], [], 1000)[0]


def in_result(plan, scale, terms):
    outs = [
        shape((in_share(plan)[0], plan.hidden), f32),
        shape((plan.side, plan.side, plan.channels), f32),
    ]
    return call(functools.partial(in_result_kernel, plan, scale), "in_result", terms, outs, [], 1000)


def to_tile(plan, strips):
    rows, cols = plan.rows, plan.cols
    me = lax.axis_index("row")
    tile = jnp.zeros((rows, *strips.shape[1:]), strips.dtype)
    own = lax.dynamic_index_in_dim(strips, me, 0, keepdims=True)
    tile = lax.dynamic_update_slice_in_dim(tile, own, me, 0)
    for dr in range(1, rows):
        target = lax.rem(me + dr, rows)
        piece = lax.dynamic_index_in_dim(strips, target, 0, keepdims=True)
        got = lax.ppermute(piece, "row", [(r, (r + dr) % rows) for r in range(rows)])
        tile = lax.dynamic_update_slice_in_dim(tile, got, lax.rem(me - dr + rows, rows), 0)
    tile = tile.reshape(plan.across, plan.height, plan.channels)
    return jnp.swapaxes(tile, 0, 1)


def one_crop(plan, norm_scale, tissue, saved, out_grad, params):
    packed, params = pack(plan, tissue, saved, out_grad, params)
    taps, w_in, w_out, conv_bias, gain, bias, b_in, scale = params
    pieces = exchange(plan, packed)
    taps_above = to_segment_below(plan, taps)
    og, xw, mask, standard, inv, gate, hidden, normed = forward(
        plan, pieces, taps, conv_bias, gain, bias, w_in, b_in
    )
    step_params, kept = (scale, gain, w_in, w_out, taps), (standard, inv, gate, mask)
    received, turned = [], None
    for _ in range(plan.segments - 1):
        own, *edges = backward_step(plan, og, received, step_params, kept)
        received = [taps_above, to_segment_below(plan, own), *send_edges(plan, edges, -1)]
        if turned is None:
            hidden, normed, _ = lax.optimization_barrier((hidden, normed, own))
            turned = turn(hidden, normed)
    hidden_t, normed_t = turned if turned is not None else turn(hidden, normed)
    upstream, branch_grad, halves, send = out_step(plan, og, received, scale, mask, hidden_t)
    out_sum = Reduction(plan, halves, send, out_share(plan), 0)
    norm_grad, halves = in_step(plan, branch_grad, w_in, w_out, gate, normed_t)
    norm_grad, _ = lax.optimization_barrier((norm_grad, out_sum.send))
    conv_grad, send, *edges = taps_step(plan, norm_grad, halves, gain, standard, inv, xw)
    in_sum = Reduction(plan, halves, send, in_share(plan)[1], taps_rows(plan))
    grad_out = out_result(plan, norm_scale, out_sum.terms())
    strips = finish(plan, upstream, conv_grad, taps, send_edges(plan, edges, 0))
    grad_in, grad_taps = in_result(plan, norm_scale, in_sum.terms())
    return to_tile(plan, strips), grad_in, grad_out, grad_taps


def per_device(
    saved_inputs,
    out_grad,
    tissue,
    conv_taps,
    conv_bias,
    norm_gain,
    norm_bias,
    w_in,
    b_in,
    w_out,
    layer_scale,
):
    crop_count, height, across, channels = out_grad.shape
    plan = Plan(
        lax.axis_size("segment"),
        lax.axis_size("row"),
        lax.axis_size("col"),
        height,
        across,
        channels,
        w_in.shape[2],
        conv_taps.shape[1],
    )
    norm_scale = 1.0 / math.sqrt(crop_count * plan.full * across * plan.cols)
    params = (conv_taps[0], w_in[0], w_out[0], conv_bias, norm_gain, norm_bias, b_in, layer_scale)
    results = [
        one_crop(plan, norm_scale, tissue[crop], saved_inputs[0, crop], out_grad[crop], params)
        for crop in range(crop_count)
    ]
    grads, *weights = zip(*results)
    grad_in, grad_out, grad_taps = (sum(w[1:], w[0]) for w in weights)
    return (jnp.stack(grads)[None], grad_in[None], grad_out[None], grad_taps[None])


def solution(mesh):
    return jax.shard_map(
        per_device,
        mesh=mesh,
        in_specs=(
            P("segment", None, "row", "col", None),
            P(None, "row", "col", None),
            P(None, "row", "col"),
            P("segment", None, None, None),
            P("segment", None),
            P("segment", None),
            P("segment", None),
            P("segment", None, None),
            P("segment", None),
            P("segment", None, None),
            P("segment", None),
        ),
        out_specs=(
            P("segment", None, "row", "col", None),
            P("segment", "col", None),
            P("segment", "col", None),
            P("segment", None, None, None),
        ),
        check_vma=False,
    )
```

```python
import functools
import math

import jax
import jax.numpy as jnp
from jax import lax
from jax.experimental import pallas as pl
from jax.experimental.pallas import tpu as pltpu
from jax.sharding import PartitionSpec as P

epsilon = 1e-06
PAD = 8
LANES = 128
VMEM_BYTES = 48 * 1024 * 1024
LINE = ("segment", "row", "col")

f32 = jnp.float32
bf16 = jnp.bfloat16


class Plan:
    def __init__(self, segments, rows, cols, height, across, channels, hidden, side):
        self.segments, self.rows, self.cols = segments, rows, cols
        self.height, self.across = height, across
        self.channels, self.hidden, self.side = channels, hidden, side
        self.margin = side // 2
        self.width = across // rows
        self.full = height * rows
        self.padded = self.width + 2 * self.margin
        self.cells = self.width * self.full
        self.part = min(256, hidden)
        self.halves = channels // LANES

    def wide(self, columns):
        return (self.halves, columns, self.full + 2 * PAD, LANES)

    def main_size(self):
        sizes = []
        for r in range(self.rows):
            low = max(0, r * self.width - self.margin)
            high = min(self.across, (r + 1) * self.width + self.margin)
            sizes.append(high - low)
        return max(sizes)

    def main_start(self, r):
        return jnp.clip(r * self.width - self.margin, 0, self.across - self.main_size())

    def needs_left(self, r):
        return r * self.width < self.margin

    def needs_right(self, r):
        return (r + 1) * self.width + self.margin > self.across

    def sides(self):
        left = [r for r in range(self.rows) if self.needs_left(r)]
        right = [r for r in range(self.rows) if self.needs_right(r)]
        if set(left) & set(right):
            return [(left, []), ([], right)]
        return [(left, right)]

    def distances(self):
        out = []
        distance = 1
        while (distance - 1) * self.width < self.margin:
            out.append((distance, min(self.width, self.margin - (distance - 1) * self.width)))
            distance += 1
        return out

    def index(self, s, r, c):
        return (s * self.rows + r) * self.cols + c

    def strip(self, s, t):
        return self.index(s, t % self.rows, t // self.rows)

    def own(self, column):
        return self.margin <= column < self.margin + self.width


def vmem():
    return pl.BlockSpec(memory_space=pltpu.VMEM)


def smem():
    return pl.BlockSpec(memory_space=pltpu.SMEM)


def shape(dims, dtype):
    return jax.ShapeDtypeStruct(tuple(dims), dtype)


def call(kernel, name, operands, outs, scratch, flops=1000):
    return pl.pallas_call(
        kernel,
        out_shape=outs,
        in_specs=[vmem()] * len(operands),
        out_specs=[vmem()] * len(outs),
        scratch_shapes=scratch,
        compiler_params=pltpu.CompilerParams(vmem_limit_bytes=VMEM_BYTES),
        cost_estimate=pl.CostEstimate(flops=flops, bytes_accessed=1000, transcendentals=0),
        name=name,
    )(*operands)


def pack_kernel(plan, x_ref, *refs):
    rows, across = plan.rows, plan.across
    outs, xt = refs[:-1], refs[-1]
    me = lax.axis_index("row")
    xt[...] = jnp.swapaxes(x_ref[...].astype(f32), 0, 1).astype(bf16)
    nx, m = plan.main_size(), plan.margin
    for dr in range(rows):
        target = lax.rem(me - dr + rows, rows)
        outs[dr][...] = xt[pl.ds(plan.main_start(target), nx)]
    for k, (left, right) in enumerate(plan.sides()):
        for dr in range(rows):
            target = lax.rem(me - dr + rows, rows)
            is_left = functools.reduce(jnp.logical_or, [target == r for r in left], jnp.bool_(False))
            outs[rows * (1 + k) + dr][...] = xt[pl.ds(jnp.where(is_left, across - m, 0), m)]


def pack(plan, x):
    rows, h, c = plan.rows, plan.height, plan.channels
    outs = [shape((plan.main_size(), h, c), bf16)] * rows
    outs += [shape((plan.margin, h, c), bf16)] * (rows * len(plan.sides()))
    return call(
        functools.partial(pack_kernel, plan), "pack", [x], outs, [pltpu.VMEM((plan.across, h, c), bf16)]
    )


def pack_upstream_kernel(plan, tissue_ref, g_ref, *refs):
    rows, across, height = plan.rows, plan.across, plan.height
    outs, gt = refs[:-1], refs[-1]
    tiles_r, tiles_c = tissue_ref.shape
    side_r, side_c = height // tiles_r, across // tiles_c
    me = lax.axis_index("row")
    row_at = lax.broadcasted_iota(jnp.int32, (height, plan.channels), 0)
    lane_at = lax.broadcasted_iota(jnp.int32, (height, plan.channels), 1)

    def slot(start):
        col_at = lane_at + start
        total = jnp.zeros((height, plan.channels), f32)
        for a in range(tiles_r):
            in_row = (row_at >= a * side_r) & (row_at < (a + 1) * side_r)
            for b in range(tiles_c):
                inside = in_row & (col_at >= b * side_c) & (col_at < (b + 1) * side_c)
                total = jnp.where(inside, tissue_ref[a, b].astype(f32), total)
        return total.astype(bf16)

    gt[...] = jnp.swapaxes(g_ref[...].astype(f32), 0, 1).astype(bf16)
    w = plan.width
    for dr in range(rows):
        target = lax.rem(me - dr + rows, rows)
        outs[dr][0:w] = gt[pl.ds(target * w, w)]
        outs[dr][w] = slot(target * w)


def pack_upstream(plan, tissue, g):
    h, c = plan.height, plan.channels
    outs = [shape((plan.width + 1, h, c), bf16)] * plan.rows
    return pl.pallas_call(
        functools.partial(pack_upstream_kernel, plan),
        out_shape=outs,
        in_specs=[smem(), vmem()],
        out_specs=[vmem()] * len(outs),
        scratch_shapes=[pltpu.VMEM((plan.across, h, c), bf16)],
        compiler_params=pltpu.CompilerParams(vmem_limit_bytes=VMEM_BYTES),
        cost_estimate=pl.CostEstimate(flops=1000, bytes_accessed=1000, transcendentals=0),
        name="pack_upstream",
    )(tissue, g)


def load_kernel(count, *refs):
    moves = [
        pltpu.make_async_copy(refs[k], refs[count + k], refs[-1].at[k]) for k in range(count)
    ]
    for move in moves:
        move.start()
    for move in moves:
        move.wait()


def load(params):
    count = len(params)
    return pl.pallas_call(
        functools.partial(load_kernel, count),
        out_shape=[shape(a.shape, a.dtype) for a in params],
        in_specs=[pl.BlockSpec(memory_space=pltpu.HBM)] * count,
        out_specs=[vmem()] * count,
        scratch_shapes=[pltpu.SemaphoreType.DMA((count,))],
        compiler_params=pltpu.CompilerParams(vmem_limit_bytes=VMEM_BYTES),
        cost_estimate=pl.CostEstimate(flops=1000, bytes_accessed=1000, transcendentals=0),
        name="load",
    )(*params)


def exchange_mains(plan, pieces):
    received = [pieces[0]]
    for dr in range(1, plan.rows):
        pairs = [((r + dr) % plan.rows, r) for r in range(plan.rows)]
        received.append(lax.ppermute(pieces[dr], "row", pairs))
    return received


def exchange_sides(plan, pieces):
    rows, cols = plan.rows, plan.cols
    received = []
    for k, (left, right) in enumerate(plan.sides()):
        for dr in range(rows):
            pairs = []
            for s in range(plan.segments):
                for r in range(rows):
                    for c in range(cols):
                        step = (-1 if r in left else 0) + (1 if r in right else 0)
                        if step != 0 and 0 <= c + step < cols:
                            source = plan.index(s, (r + dr) % rows, c + step)
                            pairs.append((source, plan.index(s, r, c)))
            received.append(lax.ppermute(pieces[rows * k + dr], LINE, pairs))
    return received


def conv_block(plan, load, row_start, half, taps_ref, flip, keep):
    side = plan.side
    lanes = pl.ds(half * LANES, LANES)
    totals = [None] * plan.width
    for i in range(side):
        rows_at = pl.ds(row_start + (side - 1 - i if flip else i), 8)
        window = [load(k, rows_at, half) if keep(k) else None for k in range(plan.padded)]
        for j in range(side):
            tap = taps_ref[i, j, :, lanes]
            move = side - 1 - j if flip else j
            for q in range(plan.width):
                if window[q + move] is not None:
                    term = tap * window[q + move]
                    totals[q] = term if totals[q] is None else totals[q] + term
    return [jnp.zeros((8, LANES), f32) if t is None else t for t in totals]


def clear_rims(ref, full):
    zeros = jnp.zeros((*ref.shape[:2], PAD, LANES), ref.dtype)
    ref[:, :, 0:PAD, :] = zeros
    ref[:, :, PAD + full : PAD + full + PAD, :] = zeros


def blocks(plan):
    return [(half, block) for half in range(plan.channels // LANES) for block in range(plan.full // 8)]


def forward_kernel(plan, *refs):
    rows, full, h = plan.rows, plan.full, plan.height
    pieces = refs[: rows * (1 + len(plan.sides()))]
    refs = refs[len(pieces) :]
    (taps_ref, conv_bias_ref, gain_ref, bias_ref, w_in_ref, b_in_ref) = refs[:6]
    (xw_ref, standard_ref, inv_ref, gate_ref, hidden_ref, normed_ref) = refs[6:12]
    wide_x, conv_ref, pre_ref = refs[12:]
    me = lax.axis_index("row")
    m, w, nx = plan.margin, plan.width, plan.main_size()

    clear_rims(wide_x, full)
    parts = [(m + plan.main_start(me), nx, pieces[dr], dr) for dr in range(rows)]
    for k, (left, right) in enumerate(plan.sides()):
        is_left = functools.reduce(jnp.logical_or, [me == r for r in left], jnp.bool_(False))
        start = jnp.where(is_left, 0, m + plan.across)
        parts += [(start, m, pieces[rows * (1 + k) + dr], dr) for dr in range(rows)]
    for start, count, piece, dr in parts:
        top = pl.multiple_of(lax.rem(me + dr, rows) * h, h)
        for half in range(plan.halves):
            wide_x[half, pl.ds(start, count), pl.ds(PAD + top, h), :] = piece[
                :, :, half * LANES : (half + 1) * LANES
            ].astype(f32)

    base = me * w
    xw_ref[...] = wide_x[:, pl.ds(base, plan.padded)]

    def load(column, rows_at, half):
        return wide_x[half, base + column, rows_at, :]

    for half, block in blocks(plan):
        lanes = pl.ds(half * LANES, LANES)
        sums = conv_block(plan, load, PAD - m + 8 * block, half, taps_ref, False, lambda k: True)
        for q in range(w):
            conv_ref[pl.ds(q * full + 8 * block, 8), lanes] = sums[q] + conv_bias_ref[:, lanes]

    for col in range(w):
        rows_at = pl.ds(col * full, full)
        conv_out = conv_ref[rows_at, :]
        average = jnp.mean(conv_out, axis=-1, keepdims=True)
        centred = conv_out - average
        spread = jnp.mean(centred * centred, axis=-1, keepdims=True)
        inv_std = lax.rsqrt(spread + epsilon)
        standard = centred * inv_std
        standard_ref[rows_at, :] = standard
        inv_ref[rows_at, :] = jnp.broadcast_to(inv_std, (full, LANES))
        normed_ref[rows_at, :] = (standard * gain_ref[...] + bias_ref[...]).astype(bf16)

    c1 = math.sqrt(2.0 / math.pi)
    c2 = c1 * 0.044715
    for n in range(plan.hidden // plan.part):
        at = pl.ds(n * plan.part, plan.part)
        pre_ref[n % 2] = (
            jnp.dot(normed_ref[...], w_in_ref[:, at], preferred_element_type=f32) + b_in_ref[:, at]
        )
        for col in range(w):
            rows_at = pl.ds(col * full, full)
            pre = pre_ref[n % 2, rows_at, :]
            square = pre * pre
            half_one = 0.5 + 0.5 * jnp.tanh(pre * (c1 + c2 * square))
            gated = pre * half_one
            slope = half_one + gated * (1.0 - half_one) * (2.0 * c1 + 6.0 * c2 * square)
            gate_ref[rows_at, at] = slope.astype(bf16)
            hidden_ref[rows_at, at] = gated.astype(bf16)


def forward(plan, pieces, taps, conv_bias, gain, bias, w_in, b_in):
    c, full, cells = plan.channels, plan.full, plan.cells
    outs = [
        shape(plan.wide(plan.padded), f32),
        shape((cells, c), f32),
        shape((cells, LANES), f32),
        shape((cells, plan.hidden), bf16),
        shape((cells, plan.hidden), bf16),
        shape((cells, c), bf16),
    ]
    scratch = [
        pltpu.VMEM(plan.wide(plan.across + 2 * plan.margin), f32),
        pltpu.VMEM((cells, c), f32),
        pltpu.VMEM((2, cells, plan.part), f32),
    ]
    return call(
        functools.partial(forward_kernel, plan),
        "forward",
        [*pieces, taps, conv_bias, gain, bias, w_in, b_in],
        outs,
        scratch,
        36 * cells * c * plan.hidden,
    )


def upstream_kernel(plan, *refs):
    pieces, (og_ref, mask_ref) = refs[:-2], refs[-2:]
    w, h, full = plan.width, plan.height, plan.full
    me = lax.axis_index("row")
    for dr, piece in enumerate(pieces):
        top = pl.multiple_of(lax.rem(me + dr, plan.rows) * h, h)
        og_ref[:, pl.ds(top, h), :] = piece[0:w]
        marks = piece[w].astype(f32)
        for l in range(w):
            at = pl.ds(pl.multiple_of(l * full + top, h), h)
            mask_ref[at, :] = jnp.broadcast_to(marks[:, l : l + 1], (h, LANES))


def upstream_strip(plan, pieces):
    outs = [shape((plan.width, plan.full, plan.channels), bf16), shape((plan.cells, LANES), f32)]
    return call(functools.partial(upstream_kernel, plan), "upstream", pieces, outs, [])


def across_lanes(value, channels):
    return jnp.concatenate([value] * (channels // LANES), axis=-1)


def fill_edges(plan, edge_ref, edges):
    clear_rims(edge_ref, plan.full)
    m, w = plan.margin, plan.width
    for k, (distance, count) in enumerate(plan.distances()):
        for start, piece in (
            (m - (distance - 1) * w - count, edges[2 * k]),
            (m + distance * w, edges[2 * k + 1]),
        ):
            for half in range(plan.halves):
                edge_ref[half, pl.ds(start, count), PAD : PAD + plan.full, :] = piece[
                    :, :, half * LANES : (half + 1) * LANES
                ].astype(f32)


def edge_sums(plan, edge_ref, taps_ref, half, block):
    def load(column, rows_at, half):
        return edge_ref[half, column, rows_at, :]

    start = PAD - plan.margin + 8 * block
    return conv_block(plan, load, start, half, taps_ref, True, lambda k: not plan.own(k))


def own_sums(plan, cg_ref, taps_ref, half, block):
    def load(column, rows_at, half):
        return cg_ref[half, column - plan.margin, rows_at, :]

    start = PAD - plan.margin + 8 * block
    return conv_block(plan, load, start, half, taps_ref, True, plan.own)


def load_upstream(plan, g_ref, og_ref, received, edge_ref):
    if received is None:
        g_ref[...] = og_ref[...]
        return
    taps_ref, main_ref, edges = received[0], received[1], received[2:]
    last = lax.axis_index("segment") == plan.segments - 1
    fill_edges(plan, edge_ref, edges)
    for half, block in blocks(plan):
        if block % 2:
            continue
        lanes = pl.ds(half * LANES, LANES)
        rows_at = pl.ds(8 * block, 16)
        parts = [edge_sums(plan, edge_ref, taps_ref, half, block + k) for k in range(2)]
        for q in range(plan.width):
            rest = jnp.concatenate([part[q] for part in parts], axis=0)
            value = (main_ref[q, rows_at, lanes].astype(f32) + rest).astype(bf16)
            g_ref[q, rows_at, lanes] = jnp.where(last, og_ref[q, rows_at, lanes], value)


def norm_back(plan, norm_grad_ref, gain_ref, standard_ref, inv_ref, cg_ref):
    full = plan.full
    clear_rims(cg_ref, full)
    for col in range(plan.width):
        rows_at = pl.ds(col * full, full)
        norm_grad = norm_grad_ref[rows_at, :] * gain_ref[...]
        standard = standard_ref[rows_at, :]
        inv_std = across_lanes(inv_ref[rows_at, :], plan.channels)
        grad = inv_std * (
            norm_grad
            - jnp.mean(norm_grad, axis=-1, keepdims=True)
            - standard * jnp.mean(norm_grad * standard, axis=-1, keepdims=True)
        )
        grad = grad.astype(bf16).astype(f32)
        for half in range(plan.halves):
            cg_ref[half, col, PAD : PAD + full, :] = grad[:, half * LANES : (half + 1) * LANES]


def contract_last(a, b):
    return lax.dot_general(a, b, (((1,), (1,)), ((), ())), preferred_element_type=f32)


def branch(plan, g_ref, scale_ref, mask_ref, bg_ref):
    full = plan.full
    for col in range(plan.width):
        rows_at = pl.ds(col * full, full)
        mask = across_lanes(mask_ref[rows_at, :], plan.channels)
        bg_ref[rows_at, :] = (mask * scale_ref[...] * g_ref[col].astype(f32)).astype(bf16)


def put_edges(plan, cg_ref, outs):
    rows_at = pl.ds(PAD, plan.full)
    for k, (distance, count) in enumerate(plan.distances()):
        for half in range(plan.halves):
            lanes = pl.ds(half * LANES, LANES)
            last = cg_ref[half, pl.ds(plan.width - count, count), rows_at, :]
            outs[2 * k][:, :, lanes] = last.astype(bf16)
            outs[2 * k + 1][:, :, lanes] = cg_ref[half, pl.ds(0, count), rows_at, :].astype(bf16)


def edge_shapes(plan):
    return [
        shape((count, plan.full, plan.channels), bf16) for _, count in plan.distances() for _ in range(2)
    ]


def send_edges(plan, edges, step):
    strips = plan.rows * plan.cols
    received = []
    for k, (distance, _) in enumerate(plan.distances()):
        for way, piece in ((distance, edges[2 * k]), (-distance, edges[2 * k + 1])):
            pairs = [
                (plan.strip(s, t), plan.strip(s + step, t + way))
                for s in range(plan.segments)
                for t in range(strips)
                if 0 <= t + way < strips and 0 <= s + step < plan.segments
            ]
            received.append(lax.ppermute(piece, LINE, pairs))
    return received


def to_segment_below(plan, value):
    return lax.ppermute(value, "segment", [(s, s - 1) for s in range(1, plan.segments)])


def step_kernel(plan, n_received, og_ref, *refs):
    received = refs[:n_received] or None
    refs = refs[n_received:]
    (scale_ref, gain_ref, w_in_ref, w_out_ref, gate_ref, mask_ref, standard_ref, inv_ref, taps_ref) = refs[:9]
    count = 2 * len(plan.distances())
    new_ref, edges = refs[9], refs[10 : 10 + count]
    g_ref, bg_ref, ng_ref, cg_ref, edge_ref = refs[10 + count :]
    load_upstream(plan, g_ref, og_ref, received, edge_ref)
    branch(plan, g_ref, scale_ref, mask_ref, bg_ref)
    for n in range(plan.hidden // plan.part):
        at = pl.ds(n * plan.part, plan.part)
        hidden_grad = contract_last(bg_ref[...], w_out_ref[at, :])
        pre_grad = (hidden_grad * gate_ref[:, at].astype(f32)).astype(bf16)
        term = contract_last(pre_grad, w_in_ref[:, at])
        ng_ref[...] = term if n == 0 else ng_ref[...] + term
    norm_back(plan, ng_ref, gain_ref, standard_ref, inv_ref, cg_ref)
    put_edges(plan, cg_ref, edges)
    for half, block in blocks(plan):
        if block % 2:
            continue
        lanes = pl.ds(half * LANES, LANES)
        rows_at = pl.ds(8 * block, 16)
        parts = [own_sums(plan, cg_ref, taps_ref, half, block + k) for k in range(2)]
        for q in range(plan.width):
            moved = jnp.concatenate([part[q] for part in parts], axis=0)
            new_ref[q, rows_at, lanes] = (g_ref[q, rows_at, lanes].astype(f32) + moved).astype(bf16)


def backward_step(plan, og, received, params, saved):
    scale, gain, w_in, w_out, taps = params
    standard, inv, gate, mask = saved
    c, full, cells = plan.channels, plan.full, plan.cells
    outs = [shape((plan.width, full, c), bf16), *edge_shapes(plan)]
    scratch = [
        pltpu.VMEM((plan.width, full, c), bf16),
        pltpu.VMEM((cells, c), bf16),
        pltpu.VMEM((cells, c), f32),
        pltpu.VMEM(plan.wide(plan.width), f32),
        pltpu.VMEM(plan.wide(plan.padded), f32),
    ]
    return call(
        functools.partial(step_kernel, plan, len(received)),
        "backward",
        [og, *received, scale, gain, w_in, w_out, gate, mask, standard, inv, taps],
        outs,
        scratch,
        4 * cells * c * plan.hidden,
    )


def turn_kernel(hidden_ref, normed_ref, hidden_t_ref, normed_t_ref):
    hidden_t_ref[...] = hidden_ref[...].astype(f32).T.astype(bf16)
    normed_t_ref[...] = normed_ref[...].astype(f32).T.astype(bf16)


def turn(hidden, normed):
    outs = [shape(hidden.shape[::-1], bf16), shape(normed.shape[::-1], bf16)]
    return call(turn_kernel, "turn", [hidden, normed], outs, [], 1000)


def out_share(plan):
    return plan.hidden // plan.cols


def in_share(plan):
    rows = plan.channels // plan.cols
    return rows, plan.hidden // plan.part * rows


def taps_rows(plan):
    return -(-(plan.side**2) // 16) * 16


def put(halves_ref, bit, share, row, value):
    half = bit if share % 2 == 0 else 1 - bit
    halves_ref[half, share // 2, pl.ds(row, value.shape[0]), :] = value


def out_kernel(plan, n_received, og_ref, *refs):
    received = refs[:n_received] or None
    scale_ref, mask_ref, hidden_t_ref, g_ref, bg_ref, halves_ref, send_ref, edge_ref = refs[n_received:]
    load_upstream(plan, g_ref, og_ref, received, edge_ref)
    branch(plan, g_ref, scale_ref, mask_ref, bg_ref)
    bit = lax.rem(lax.axis_index("col"), 2)
    rows = out_share(plan)
    piece = min(plan.part, rows)
    for n in range(plan.hidden // plan.part):
        at = pl.ds(n * plan.part, plan.part)
        grad_out = jnp.dot(hidden_t_ref[at, :], bg_ref[...], preferred_element_type=f32)
        for start in range(0, plan.part, piece):
            unit = n * plan.part + start
            put(halves_ref, bit, unit // rows, unit % rows, grad_out[start : start + piece])
    for u in range(plan.cols // 2):
        send_ref[pl.ds(u * rows, rows), :] = halves_ref[1, u].astype(bf16)


def out_step(plan, og, received, scale, mask, hidden_t):
    c, full, cells, half = plan.channels, plan.full, plan.cells, plan.cols // 2
    rows = out_share(plan)
    outs = [
        shape((plan.width, full, c), bf16),
        shape((cells, c), bf16),
        shape((2, half, rows, c), f32),
        shape((half * rows, c), bf16),
    ]
    return call(
        functools.partial(out_kernel, plan, len(received)),
        "grad_out",
        [og, *received, scale, mask, hidden_t],
        outs,
        [pltpu.VMEM(plan.wide(plan.padded), f32)],
        2 * cells * c * plan.hidden,
    )


def in_kernel(plan, bg_ref, w_in_ref, w_out_ref, gate_ref, normed_t_ref, ng_ref, halves_ref):
    bit = lax.rem(lax.axis_index("col"), 2)
    rows, _ = in_share(plan)
    for n in range(plan.hidden // plan.part):
        at = pl.ds(n * plan.part, plan.part)
        hidden_grad = contract_last(bg_ref[...], w_out_ref[at, :])
        pre_grad = (hidden_grad * gate_ref[:, at].astype(f32)).astype(bf16)
        term = contract_last(pre_grad, w_in_ref[:, at])
        ng_ref[...] = term if n == 0 else ng_ref[...] + term
        grad_in = jnp.dot(normed_t_ref[...], pre_grad, preferred_element_type=f32)
        for share in range(plan.cols):
            put(halves_ref, bit, share, n * rows, grad_in[share * rows : (share + 1) * rows])


def in_step(plan, bg, w_in, w_out, gate, normed_t):
    c, cells = plan.channels, plan.cells
    outs = [shape((cells, c), f32), shape((2, plan.cols // 2, in_share(plan)[1], c), f32)]
    return call(
        functools.partial(in_kernel, plan),
        "grad_in",
        [bg, w_in, w_out, gate, normed_t],
        outs,
        [],
        6 * cells * c * plan.hidden,
    )


def taps_kernel(plan, ng_ref, halves_ref, gain_ref, standard_ref, inv_ref, xw_ref, cg_ref, send_ref, *edges):
    full, width, side = plan.full, plan.width, plan.side
    _, share_rows = in_share(plan)
    norm_back(plan, ng_ref, gain_ref, standard_ref, inv_ref, cg_ref)
    put_edges(plan, cg_ref, edges)
    count = plan.cols // 2
    for u in range(count):
        send_ref[pl.ds(u * share_rows, share_rows), :] = halves_ref[1, u].astype(bf16)
    rows = []
    for i in range(side):
        pieces = [[] for _ in range(side)]
        for half in range(plan.halves):
            totals = [jnp.zeros((8, LANES), f32) for _ in range(side)]
            for block in range(full // 8):
                window = xw_ref[half, :, pl.ds(PAD - plan.margin + i + 8 * block, 8), :]
                grad = cg_ref[half, :, pl.ds(PAD + 8 * block, 8), :]
                for j in range(side):
                    totals[j] = totals[j] + jnp.sum(window[j : j + width] * grad, axis=0)
            for j in range(side):
                pieces[j].append(jnp.sum(totals[j], axis=0, keepdims=True))
        rows += [jnp.concatenate(p, axis=-1) for p in pieces]
    rows.append(jnp.zeros((taps_rows(plan) - side**2, plan.channels), f32))
    at = pl.ds(count * share_rows, taps_rows(plan))
    send_ref[at, :] = jnp.concatenate(rows, axis=0).astype(bf16)


def taps_step(plan, norm_grad, halves, gain, standard, inv, xw):
    c, full = plan.channels, plan.full
    outs = [
        shape(plan.wide(plan.width), f32),
        shape((plan.cols // 2 * in_share(plan)[1] + taps_rows(plan), c), bf16),
        *edge_shapes(plan),
    ]
    return call(
        functools.partial(taps_kernel, plan),
        "grad_taps",
        [norm_grad, halves, gain, standard, inv, xw],
        outs,
        [],
        2 * plan.cells * c * plan.side**2,
    )


def finish_kernel(plan, g_ref, cg_ref, taps_ref, *refs):
    edges, (new_ref, edge_ref) = refs[:-2], refs[-2:]
    fill_edges(plan, edge_ref, edges)
    for half, block in blocks(plan):
        if block % 2:
            continue
        lanes = pl.ds(half * LANES, LANES)
        own = [own_sums(plan, cg_ref, taps_ref, half, block + k) for k in range(2)]
        rest = [edge_sums(plan, edge_ref, taps_ref, half, block + k) for k in range(2)]
        r, at = divmod(8 * block, plan.height)
        for q in range(plan.width):
            moved = jnp.concatenate([own[k][q] + rest[k][q] for k in range(2)], axis=0)
            upstream = g_ref[q, pl.ds(8 * block, 16), lanes].astype(f32)
            new_ref[r, q, pl.ds(at, 16), lanes] = (upstream + moved).astype(bf16)


def finish(plan, upstream, conv_grad, taps, edges):
    c = plan.channels
    return call(
        functools.partial(finish_kernel, plan),
        "finish",
        [upstream, conv_grad, taps, *edges],
        [shape((plan.rows, plan.width, plan.height, c), bf16)],
        [pltpu.VMEM(plan.wide(plan.padded), f32)],
        2 * plan.cells * c * plan.side**2,
    )[0]


def swap(value, axis, bit):
    size = lax.axis_size(axis)
    return lax.ppermute(value, axis, [(i, i ^ bit) for i in range(size)])


def combine_kernel(bit, share_rows, extra, keep_ref, sent_ref, got_ref, send_ref, next_ref):
    count = keep_ref.shape[1]
    mine = lax.rem(lax.axis_index("col") // bit, 2)
    for u in range(count // 2):
        for half in range(2):
            share = 2 * u + (mine if half == 0 else 1 - mine)
            at = pl.ds(pl.multiple_of(share * share_rows, 16), share_rows)
            value = keep_ref[0, share] + got_ref[at, :].astype(f32)
            if half == 0:
                next_ref[0, u] = value
            else:
                send_ref[pl.ds(u * share_rows, share_rows), :] = value.astype(bf16)
    if extra:
        old = pl.ds(count * share_rows, extra)
        new = pl.ds(count // 2 * share_rows, extra)
        send_ref[new, :] = (sent_ref[old, :].astype(f32) + got_ref[old, :].astype(f32)).astype(bf16)


def close_kernel(share_rows, extra, keep_ref, sent_ref, got_ref, out_ref):
    at = pl.ds(0, share_rows)
    out_ref[at, :] = (keep_ref[0, 0] + got_ref[at, :].astype(f32)).astype(bf16)
    if extra:
        rest = pl.ds(share_rows, extra)
        out_ref[rest, :] = (sent_ref[rest, :].astype(f32) + got_ref[rest, :].astype(f32)).astype(bf16)


class Reduction:
    def __init__(self, plan, halves, send, share_rows, extra):
        self.plan, self.share_rows, self.extra = plan, share_rows, extra
        self.keep, self.send, self.bit = halves, send, 1
        self.total = None
        if plan.cols > 2:
            self.next_stage()

    def next_stage(self):
        c = self.plan.channels
        got = swap(self.send, "col", self.bit)
        self.bit *= 2
        count = self.keep.shape[1] // 2
        self.send, self.keep = call(
            functools.partial(combine_kernel, self.bit, self.share_rows, self.extra),
            "combine",
            [self.keep, self.send, got],
            [
                shape((count * self.share_rows + self.extra, c), bf16),
                shape((1, count, self.share_rows, c), f32),
            ],
            [],
            1000,
        )

    def close(self, after=None):
        plan = self.plan
        while 2 * self.bit < plan.cols:
            self.next_stage()
        got = swap(self.send, "col", self.bit)
        if after is not None:
            got, _ = lax.optimization_barrier((got, after))
        self.total = call(
            functools.partial(close_kernel, self.share_rows, self.extra),
            "close",
            [self.keep, self.send, got],
            [shape((self.share_rows + self.extra, plan.channels), bf16)],
            [],
        )[0]

    def terms(self):
        plan, total = self.plan, self.total
        terms = [total]
        bit = 1
        while bit < plan.rows:
            terms = [total, swap(total, "row", bit)]
            bit *= 2
            if bit < plan.rows:
                total = (terms[0].astype(f32) + terms[1].astype(f32)).astype(bf16)
        return terms


def read(refs, scale, start, count):
    return scale * sum(ref[pl.ds(start, count), :].astype(f32) for ref in refs)


def out_result_kernel(plan, scale, *refs):
    refs[-1][...] = read(refs[:-1], scale, 0, out_share(plan))


def in_result_kernel(plan, scale, *refs):
    terms, (in_ref, taps_ref) = refs[:-2], refs[-2:]
    rows, share_rows = in_share(plan)
    for n in range(plan.hidden // plan.part):
        in_ref[:, pl.ds(n * plan.part, plan.part)] = read(terms, scale, n * rows, rows)
    sums = read(terms, scale, share_rows, taps_rows(plan))
    for i in range(plan.side):
        for j in range(plan.side):
            row = i * plan.side + j
            taps_ref[i, j] = sums[row : row + 1]


def out_result(plan, scale, terms):
    kernel = functools.partial(out_result_kernel, plan, scale)
    return call(kernel, "out_result", terms, [shape((out_share(plan), plan.channels), f32)], [], 1000)[0]


def in_result(plan, scale, terms):
    outs = [
        shape((in_share(plan)[0], plan.hidden), f32),
        shape((plan.side, plan.side, 1, plan.channels), f32),
    ]
    return call(functools.partial(in_result_kernel, plan, scale), "in_result", terms, outs, [], 1000)


def to_tile(plan, strips):
    rows, cols = plan.rows, plan.cols
    me = lax.axis_index("row")
    tile = jnp.zeros((rows, *strips.shape[1:]), strips.dtype)
    own = lax.dynamic_index_in_dim(strips, me, 0, keepdims=True)
    tile = lax.dynamic_update_slice_in_dim(tile, own, me, 0)
    for dr in range(1, rows):
        target = lax.rem(me + dr, rows)
        piece = lax.dynamic_index_in_dim(strips, target, 0, keepdims=True)
        got = lax.ppermute(piece, "row", [(r, (r + dr) % rows) for r in range(rows)])
        tile = lax.dynamic_update_slice_in_dim(tile, got, lax.rem(me - dr + rows, rows), 0)
    tile = tile.reshape(plan.across, plan.height, plan.channels)
    return jnp.swapaxes(tile, 0, 1)


def one_crop(plan, norm_scale, tissue, saved, out_grad, params):
    packed = pack(plan, saved)
    mains, sides = packed[: plan.rows], packed[plan.rows :]
    sides, mains = lax.optimization_barrier((exchange_sides(plan, sides), mains))
    pieces = exchange_mains(plan, mains) + sides
    upstream = exchange_mains(plan, pack_upstream(plan, tissue, out_grad))
    taps_above = to_segment_below(plan, params[0])
    taps, w_in, w_out, conv_bias, gain, bias, b_in, scale = load(params)
    xw, standard, inv, gate, hidden, normed = forward(
        plan, pieces, taps, conv_bias, gain, bias, w_in, b_in
    )
    og, mask, taps_above = lax.optimization_barrier((*upstream_strip(plan, upstream), taps_above))
    step_params, kept = (scale, gain, w_in, w_out, taps), (standard, inv, gate, mask)
    received, turned = [], None
    for _ in range(plan.segments - 1):
        own, *edges = backward_step(plan, og, received, step_params, kept)
        received = [taps_above, to_segment_below(plan, own), *send_edges(plan, edges, -1)]
        if turned is None:
            hidden, normed, _ = lax.optimization_barrier((hidden, normed, own))
            turned = turn(hidden, normed)
    hidden_t, normed_t = turned if turned is not None else turn(hidden, normed)
    upstream, branch_grad, halves, send = out_step(plan, og, received, scale, mask, hidden_t)
    out_sum = Reduction(plan, halves, send, out_share(plan), 0)
    norm_grad, halves = in_step(plan, branch_grad, w_in, w_out, gate, normed_t)
    norm_grad, _ = lax.optimization_barrier((norm_grad, out_sum.send))
    conv_grad, send, *edges = taps_step(plan, norm_grad, halves, gain, standard, inv, xw)
    in_sum = Reduction(plan, halves, send, in_share(plan)[1], taps_rows(plan))
    out_sum.close(in_sum.send)
    grad_out = out_result(plan, norm_scale, out_sum.terms())
    edges, _, _ = lax.optimization_barrier((edges, in_sum.send, out_sum.total))
    strips = finish(plan, upstream, conv_grad, taps, send_edges(plan, edges, 0))
    in_sum.close()
    grad_in, grad_taps = in_result(plan, norm_scale, in_sum.terms())
    return to_tile(plan, strips), grad_in, grad_out, grad_taps


def per_device(
    saved_inputs,
    out_grad,
    tissue,
    conv_taps,
    conv_bias,
    norm_gain,
    norm_bias,
    w_in,
    b_in,
    w_out,
    layer_scale,
):
    crop_count, height, across, channels = out_grad.shape
    plan = Plan(
        lax.axis_size("segment"),
        lax.axis_size("row"),
        lax.axis_size("col"),
        height,
        across,
        channels,
        w_in.shape[2],
        conv_taps.shape[1],
    )
    norm_scale = 1.0 / math.sqrt(crop_count * plan.full * across * plan.cols)
    params = (conv_taps.transpose(1, 2, 0, 3), w_in[0], w_out[0], conv_bias, norm_gain, norm_bias, b_in, layer_scale)
    results = [
        one_crop(plan, norm_scale, tissue[crop], saved_inputs[0, crop], out_grad[crop], params)
        for crop in range(crop_count)
    ]
    grads, *weights = zip(*results)
    grad_in, grad_out, grad_taps = (sum(w[1:], w[0]) for w in weights)
    return (jnp.stack(grads)[None], grad_in[None], grad_out[None], grad_taps.transpose(2, 0, 1, 3))


def solution(mesh):
    return jax.shard_map(
        per_device,
        mesh=mesh,
        in_specs=(
            P("segment", None, "row", "col", None),
            P(None, "row", "col", None),
            P(None, "row", "col"),
            P("segment", None, None, None),
            P("segment", None),
            P("segment", None),
            P("segment", None),
            P("segment", None, None),
            P("segment", None),
            P("segment", None, None),
            P("segment", None),
        ),
        out_specs=(
            P("segment", None, "row", "col", None),
            P("segment", "col", None),
            P("segment", "col", None),
            P("segment", None, None, None),
        ),
        check_vma=False,
    )
```

```python
import functools
import math

import jax
import jax.numpy as jnp
from jax import lax
from jax.experimental import pallas as pl
from jax.experimental.pallas import tpu as pltpu
from jax.sharding import PartitionSpec as P

epsilon = 1e-06
PAD = 8
LANES = 128
VMEM_BYTES = 48 * 1024 * 1024
LINE = ("segment", "row", "col")

f32 = jnp.float32
bf16 = jnp.bfloat16


class Plan:
    def __init__(self, segments, rows, cols, height, across, channels, hidden, side):
        self.segments, self.rows, self.cols = segments, rows, cols
        self.height, self.across = height, across
        self.channels, self.hidden, self.side = channels, hidden, side
        self.margin = side // 2
        self.width = across // rows
        self.full = height * rows
        self.padded = self.width + 2 * self.margin
        self.cells = self.width * self.full
        self.part = min(256, hidden)
        self.halves = channels // LANES

    def wide(self, columns):
        return (self.halves, columns, self.full + 2 * PAD, LANES)

    def main_size(self):
        sizes = []
        for r in range(self.rows):
            low = max(0, r * self.width - self.margin)
            high = min(self.across, (r + 1) * self.width + self.margin)
            sizes.append(high - low)
        return max(sizes)

    def turned(self, place, c):
        return place + (c % 2) * (self.rows - 1 - 2 * place)

    def place(self, r):
        return self.turned(r, lax.axis_index("col"))

    def main_start(self, place):
        return jnp.clip(place * self.width - self.margin, 0, self.across - self.main_size())

    def sides(self):
        left = [u for u in range(self.rows) if u * self.width < self.margin]
        right = [u for u in range(self.rows) if (u + 1) * self.width + self.margin > self.across]
        if set(left) & set(right):
            return [(left, []), ([], right)]
        return [(left, right)]

    def distances(self):
        out = []
        distance = 1
        while (distance - 1) * self.width < self.margin:
            out.append((distance, min(self.width, self.margin - (distance - 1) * self.width)))
            distance += 1
        return out

    def index(self, s, r, c):
        return (s * self.rows + r) * self.cols + c

    def strip(self, s, t):
        c = t // self.rows
        return self.index(s, self.turned(t % self.rows, c), c)

    def own(self, column):
        return self.margin <= column < self.margin + self.width


def vmem():
    return pl.BlockSpec(memory_space=pltpu.VMEM)


def smem():
    return pl.BlockSpec(memory_space=pltpu.SMEM)


def shape(dims, dtype):
    return jax.ShapeDtypeStruct(tuple(dims), dtype)


def call(kernel, name, operands, outs, scratch, flops=1000):
    return pl.pallas_call(
        kernel,
        out_shape=outs,
        in_specs=[vmem()] * len(operands),
        out_specs=[vmem()] * len(outs),
        scratch_shapes=scratch,
        compiler_params=pltpu.CompilerParams(vmem_limit_bytes=VMEM_BYTES),
        cost_estimate=pl.CostEstimate(flops=flops, bytes_accessed=1000, transcendentals=0),
        name=name,
    )(*operands)


def pack_kernel(plan, x_ref, *refs):
    outs, xt = refs[:-1], refs[-1]
    me = lax.axis_index("row")
    xt[...] = jnp.swapaxes(x_ref[...].astype(f32), 0, 1).astype(bf16)
    for dr in range(plan.rows):
        target = plan.place(lax.rem(me - dr + plan.rows, plan.rows))
        outs[dr][...] = xt[pl.ds(plan.main_start(target), plan.main_size())]


def pack(plan, x):
    h, c = plan.height, plan.channels
    outs = [shape((plan.main_size(), h, c), bf16)] * plan.rows
    return call(
        functools.partial(pack_kernel, plan), "pack", [x], outs, [pltpu.VMEM((plan.across, h, c), bf16)]
    )


def among(value, numbers):
    return functools.reduce(jnp.logical_or, [value == k for k in numbers], jnp.bool_(False))


def pack_sides_kernel(plan, *refs):
    pieces, outs = refs[: plan.rows], refs[plan.rows :]
    me = lax.axis_index("row")
    m, nx = plan.margin, plan.main_size()
    for out, (left, right) in zip(outs, plan.sides()):
        is_left = among(plan.place(me), left)
        for dr, piece in enumerate(pieces):
            top = pl.multiple_of(lax.rem(me + dr, plan.rows) * plan.height, plan.height)
            out[:, pl.ds(top, plan.height), :] = jnp.where(is_left, piece[0:m], piece[nx - m : nx])


def pack_sides(plan, pieces):
    outs = [shape((plan.margin, plan.full, plan.channels), bf16)] * len(plan.sides())
    return call(functools.partial(pack_sides_kernel, plan), "pack_sides", pieces, outs, [])


def pack_upstream_kernel(plan, tissue_ref, g_ref, *refs):
    rows, across, height = plan.rows, plan.across, plan.height
    outs, gt = refs[:-1], refs[-1]
    tiles_r, tiles_c = tissue_ref.shape
    side_r, side_c = height // tiles_r, across // tiles_c
    me = lax.axis_index("row")
    row_at = lax.broadcasted_iota(jnp.int32, (height, plan.channels), 0)
    lane_at = lax.broadcasted_iota(jnp.int32, (height, plan.channels), 1)

    def slot(start):
        col_at = lane_at + start
        total = jnp.zeros((height, plan.channels), f32)
        for a in range(tiles_r):
            in_row = (row_at >= a * side_r) & (row_at < (a + 1) * side_r)
            for b in range(tiles_c):
                inside = in_row & (col_at >= b * side_c) & (col_at < (b + 1) * side_c)
                total = jnp.where(inside, tissue_ref[a, b].astype(f32), total)
        return total.astype(bf16)

    gt[...] = jnp.swapaxes(g_ref[...].astype(f32), 0, 1).astype(bf16)
    w = plan.width
    for dr in range(rows):
        target = plan.place(lax.rem(me - dr + rows, rows))
        outs[dr][0:w] = gt[pl.ds(target * w, w)]
        outs[dr][w] = slot(target * w)


def pack_upstream(plan, tissue, g):
    h, c = plan.height, plan.channels
    outs = [shape((plan.width + 1, h, c), bf16)] * plan.rows
    return pl.pallas_call(
        functools.partial(pack_upstream_kernel, plan),
        out_shape=outs,
        in_specs=[smem(), vmem()],
        out_specs=[vmem()] * len(outs),
        scratch_shapes=[pltpu.VMEM((plan.across, h, c), bf16)],
        compiler_params=pltpu.CompilerParams(vmem_limit_bytes=VMEM_BYTES),
        cost_estimate=pl.CostEstimate(flops=1000, bytes_accessed=1000, transcendentals=0),
        name="pack_upstream",
    )(tissue, g)


def load_kernel(count, *refs):
    moves = [
        pltpu.make_async_copy(refs[k], refs[count + k], refs[-1].at[k]) for k in range(count)
    ]
    for move in moves:
        move.start()
    for move in moves:
        move.wait()


def load(params):
    count = len(params)
    return pl.pallas_call(
        functools.partial(load_kernel, count),
        out_shape=[shape(a.shape, a.dtype) for a in params],
        in_specs=[pl.BlockSpec(memory_space=pltpu.HBM)] * count,
        out_specs=[vmem()] * count,
        scratch_shapes=[pltpu.SemaphoreType.DMA((count,))],
        compiler_params=pltpu.CompilerParams(vmem_limit_bytes=VMEM_BYTES),
        cost_estimate=pl.CostEstimate(flops=1000, bytes_accessed=1000, transcendentals=0),
        name="load",
    )(*params)


def exchange_mains(plan, pieces):
    received = [pieces[0]]
    for dr in range(1, plan.rows):
        pairs = [((r + dr) % plan.rows, r) for r in range(plan.rows)]
        received.append(lax.ppermute(pieces[dr], "row", pairs))
    return received


def exchange_sides(plan, pieces):
    rows, cols = plan.rows, plan.cols
    received = []
    for piece, (left, right) in zip(pieces, plan.sides()):
        pairs = []
        for s in range(plan.segments):
            for c in range(cols):
                for u in range(rows):
                    step = (-1 if u in left else 0) + (1 if u in right else 0)
                    if step != 0 and 0 <= c + step < cols:
                        source = plan.index(s, plan.turned(rows - 1 - u, c + step), c + step)
                        pairs.append((source, plan.index(s, plan.turned(u, c), c)))
        received.append(lax.ppermute(piece, LINE, pairs))
    return received


def conv_block(plan, load, row_start, half, taps_ref, flip, keep):
    side = plan.side
    lanes = pl.ds(half * LANES, LANES)
    totals = [None] * plan.width
    for i in range(side):
        rows_at = pl.ds(row_start + (side - 1 - i if flip else i), 8)
        window = [load(k, rows_at, half) if keep(k) else None for k in range(plan.padded)]
        for j in range(side):
            tap = taps_ref[i, j, :, lanes]
            move = side - 1 - j if flip else j
            for q in range(plan.width):
                if window[q + move] is not None:
                    term = tap * window[q + move]
                    totals[q] = term if totals[q] is None else totals[q] + term
    return [jnp.zeros((8, LANES), f32) if t is None else t for t in totals]


def clear_rims(ref, full):
    zeros = jnp.zeros((*ref.shape[:2], PAD, LANES), ref.dtype)
    ref[:, :, 0:PAD, :] = zeros
    ref[:, :, PAD + full : PAD + full + PAD, :] = zeros


def blocks(plan):
    return [(half, block) for half in range(plan.channels // LANES) for block in range(plan.full // 8)]


def forward_kernel(plan, *refs):
    rows, full, h = plan.rows, plan.full, plan.height
    mains, sides = refs[:rows], refs[rows : rows + len(plan.sides())]
    refs = refs[rows + len(sides) :]
    (taps_ref, conv_bias_ref, gain_ref, bias_ref, w_in_ref, b_in_ref) = refs[:6]
    (xw_ref, standard_ref, inv_ref, gate_ref, hidden_ref, normed_ref) = refs[6:12]
    wide_x, conv_ref, pre_ref = refs[12:]
    me = lax.axis_index("row")
    place = plan.place(me)
    m, w, nx = plan.margin, plan.width, plan.main_size()

    clear_rims(wide_x, full)
    parts = []
    for dr, piece in enumerate(mains):
        top = pl.multiple_of(lax.rem(me + dr, rows) * h, h)
        parts.append((m + plan.main_start(place), nx, top, h, piece))
    for piece, (left, right) in zip(sides, plan.sides()):
        parts.append((jnp.where(among(place, left), 0, m + plan.across), m, 0, full, piece))
    for start, count, top, height, piece in parts:
        for half in range(plan.halves):
            wide_x[half, pl.ds(start, count), pl.ds(PAD + top, height), :] = piece[
                :, :, half * LANES : (half + 1) * LANES
            ].astype(f32)

    base = place * w
    xw_ref[...] = wide_x[:, pl.ds(base, plan.padded)]

    def load(column, rows_at, half):
        return wide_x[half, base + column, rows_at, :]

    for half, block in blocks(plan):
        lanes = pl.ds(half * LANES, LANES)
        sums = conv_block(plan, load, PAD - m + 8 * block, half, taps_ref, False, lambda k: True)
        for q in range(w):
            conv_ref[pl.ds(q * full + 8 * block, 8), lanes] = sums[q] + conv_bias_ref[:, lanes]

    for col in range(w):
        rows_at = pl.ds(col * full, full)
        conv_out = conv_ref[rows_at, :]
        average = jnp.mean(conv_out, axis=-1, keepdims=True)
        centred = conv_out - average
        spread = jnp.mean(centred * centred, axis=-1, keepdims=True)
        inv_std = lax.rsqrt(spread + epsilon)
        standard = centred * inv_std
        standard_ref[rows_at, :] = standard
        inv_ref[rows_at, :] = jnp.broadcast_to(inv_std, (full, LANES))
        normed_ref[rows_at, :] = (standard * gain_ref[...] + bias_ref[...]).astype(bf16)

    c1 = math.sqrt(2.0 / math.pi)
    c2 = c1 * 0.044715
    for n in range(plan.hidden // plan.part):
        at = pl.ds(n * plan.part, plan.part)
        pre_ref[n % 2] = (
            jnp.dot(normed_ref[...], w_in_ref[:, at], preferred_element_type=f32) + b_in_ref[:, at]
        )
        for col in range(w):
            rows_at = pl.ds(col * full, full)
            pre = pre_ref[n % 2, rows_at, :]
            square = pre * pre
            half_one = 0.5 + 0.5 * jnp.tanh(pre * (c1 + c2 * square))
            gated = pre * half_one
            slope = half_one + gated * (1.0 - half_one) * (2.0 * c1 + 6.0 * c2 * square)
            gate_ref[rows_at, at] = slope.astype(bf16)
            hidden_ref[rows_at, at] = gated.astype(bf16)


def forward(plan, pieces, taps, conv_bias, gain, bias, w_in, b_in):
    c, full, cells = plan.channels, plan.full, plan.cells
    outs = [
        shape(plan.wide(plan.padded), f32),
        shape((cells, c), f32),
        shape((cells, LANES), f32),
        shape((cells, plan.hidden), bf16),
        shape((cells, plan.hidden), bf16),
        shape((cells, c), bf16),
    ]
    scratch = [
        pltpu.VMEM(plan.wide(plan.across + 2 * plan.margin), f32),
        pltpu.VMEM((cells, c), f32),
        pltpu.VMEM((2, cells, plan.part), f32),
    ]
    return call(
        functools.partial(forward_kernel, plan),
        "forward",
        [*pieces, taps, conv_bias, gain, bias, w_in, b_in],
        outs,
        scratch,
        36 * cells * c * plan.hidden,
    )


def upstream_kernel(plan, *refs):
    pieces, (og_ref, mask_ref) = refs[:-2], refs[-2:]
    w, h, full = plan.width, plan.height, plan.full
    me = lax.axis_index("row")
    for dr, piece in enumerate(pieces):
        top = pl.multiple_of(lax.rem(me + dr, plan.rows) * h, h)
        og_ref[:, pl.ds(top, h), :] = piece[0:w]
        marks = piece[w].astype(f32)
        for l in range(w):
            at = pl.ds(pl.multiple_of(l * full + top, h), h)
            mask_ref[at, :] = jnp.broadcast_to(marks[:, l : l + 1], (h, LANES))


def upstream_strip(plan, pieces):
    outs = [shape((plan.width, plan.full, plan.channels), bf16), shape((plan.cells, LANES), f32)]
    return call(functools.partial(upstream_kernel, plan), "upstream", pieces, outs, [])


def across_lanes(value, channels):
    return jnp.concatenate([value] * (channels // LANES), axis=-1)


def fill_edges(plan, edge_ref, edges):
    clear_rims(edge_ref, plan.full)
    m, w = plan.margin, plan.width
    for k, (distance, count) in enumerate(plan.distances()):
        for start, piece in (
            (m - (distance - 1) * w - count, edges[2 * k]),
            (m + distance * w, edges[2 * k + 1]),
        ):
            for half in range(plan.halves):
                edge_ref[half, pl.ds(start, count), PAD : PAD + plan.full, :] = piece[
                    :, :, half * LANES : (half + 1) * LANES
                ].astype(f32)


def edge_sums(plan, edge_ref, taps_ref, half, block):
    def load(column, rows_at, half):
        return edge_ref[half, column, rows_at, :]

    start = PAD - plan.margin + 8 * block
    return conv_block(plan, load, start, half, taps_ref, True, lambda k: not plan.own(k))


def own_sums(plan, cg_ref, taps_ref, half, block):
    def load(column, rows_at, half):
        return cg_ref[half, column - plan.margin, rows_at, :]

    start = PAD - plan.margin + 8 * block
    return conv_block(plan, load, start, half, taps_ref, True, plan.own)


def load_upstream(plan, g_ref, og_ref, received, edge_ref):
    if received is None:
        g_ref[...] = og_ref[...]
        return
    taps_ref, main_ref, edges = received[0], received[1], received[2:]
    last = lax.axis_index("segment") == plan.segments - 1
    fill_edges(plan, edge_ref, edges)
    for half, block in blocks(plan):
        if block % 2:
            continue
        lanes = pl.ds(half * LANES, LANES)
        rows_at = pl.ds(8 * block, 16)
        parts = [edge_sums(plan, edge_ref, taps_ref, half, block + k) for k in range(2)]
        for q in range(plan.width):
            rest = jnp.concatenate([part[q] for part in parts], axis=0)
            value = (main_ref[q, rows_at, lanes].astype(f32) + rest).astype(bf16)
            g_ref[q, rows_at, lanes] = jnp.where(last, og_ref[q, rows_at, lanes], value)


def norm_back(plan, norm_grad_ref, gain_ref, standard_ref, inv_ref, cg_ref):
    full = plan.full
    clear_rims(cg_ref, full)
    for col in range(plan.width):
        rows_at = pl.ds(col * full, full)
        norm_grad = norm_grad_ref[rows_at, :] * gain_ref[...]
        standard = standard_ref[rows_at, :]
        inv_std = across_lanes(inv_ref[rows_at, :], plan.channels)
        grad = inv_std * (
            norm_grad
            - jnp.mean(norm_grad, axis=-1, keepdims=True)
            - standard * jnp.mean(norm_grad * standard, axis=-1, keepdims=True)
        )
        grad = grad.astype(bf16).astype(f32)
        for half in range(plan.halves):
            cg_ref[half, col, PAD : PAD + full, :] = grad[:, half * LANES : (half + 1) * LANES]


def contract_last(a, b):
    return lax.dot_general(a, b, (((1,), (1,)), ((), ())), preferred_element_type=f32)


def branch(plan, g_ref, scale_ref, mask_ref, bg_ref):
    full = plan.full
    for col in range(plan.width):
        rows_at = pl.ds(col * full, full)
        mask = across_lanes(mask_ref[rows_at, :], plan.channels)
        bg_ref[rows_at, :] = (mask * scale_ref[...] * g_ref[col].astype(f32)).astype(bf16)


def put_edges(plan, cg_ref, outs):
    rows_at = pl.ds(PAD, plan.full)
    for k, (distance, count) in enumerate(plan.distances()):
        for half in range(plan.halves):
            lanes = pl.ds(half * LANES, LANES)
            last = cg_ref[half, pl.ds(plan.width - count, count), rows_at, :]
            outs[2 * k][:, :, lanes] = last.astype(bf16)
            outs[2 * k + 1][:, :, lanes] = cg_ref[half, pl.ds(0, count), rows_at, :].astype(bf16)


def edge_shapes(plan):
    return [
        shape((count, plan.full, plan.channels), bf16) for _, count in plan.distances() for _ in range(2)
    ]


def send_edges(plan, edges, step):
    strips = plan.rows * plan.cols
    received = []
    for k, (distance, _) in enumerate(plan.distances()):
        for way, piece in ((distance, edges[2 * k]), (-distance, edges[2 * k + 1])):
            pairs = [
                (plan.strip(s, t), plan.strip(s + step, t + way))
                for s in range(plan.segments)
                for t in range(strips)
                if 0 <= t + way < strips and 0 <= s + step < plan.segments
            ]
            received.append(lax.ppermute(piece, LINE, pairs))
    return received


def to_segment_below(plan, value):
    return lax.ppermute(value, "segment", [(s, s - 1) for s in range(1, plan.segments)])


def step_kernel(plan, n_received, og_ref, *refs):
    received = refs[:n_received] or None
    refs = refs[n_received:]
    (scale_ref, gain_ref, w_in_ref, w_out_ref, gate_ref, mask_ref, standard_ref, inv_ref, taps_ref) = refs[:9]
    count = 2 * len(plan.distances())
    new_ref, edges = refs[9], refs[10 : 10 + count]
    g_ref, bg_ref, ng_ref, cg_ref, edge_ref = refs[10 + count :]
    load_upstream(plan, g_ref, og_ref, received, edge_ref)
    branch(plan, g_ref, scale_ref, mask_ref, bg_ref)
    for n in range(plan.hidden // plan.part):
        at = pl.ds(n * plan.part, plan.part)
        hidden_grad = contract_last(bg_ref[...], w_out_ref[at, :])
        pre_grad = (hidden_grad * gate_ref[:, at].astype(f32)).astype(bf16)
        term = contract_last(pre_grad, w_in_ref[:, at])
        ng_ref[...] = term if n == 0 else ng_ref[...] + term
    norm_back(plan, ng_ref, gain_ref, standard_ref, inv_ref, cg_ref)
    put_edges(plan, cg_ref, edges)
    for half, block in blocks(plan):
        if block % 2:
            continue
        lanes = pl.ds(half * LANES, LANES)
        rows_at = pl.ds(8 * block, 16)
        parts = [own_sums(plan, cg_ref, taps_ref, half, block + k) for k in range(2)]
        for q in range(plan.width):
            moved = jnp.concatenate([part[q] for part in parts], axis=0)
            new_ref[q, rows_at, lanes] = (g_ref[q, rows_at, lanes].astype(f32) + moved).astype(bf16)


def backward_step(plan, og, received, params, saved):
    scale, gain, w_in, w_out, taps = params
    standard, inv, gate, mask = saved
    c, full, cells = plan.channels, plan.full, plan.cells
    outs = [shape((plan.width, full, c), bf16), *edge_shapes(plan)]
    scratch = [
        pltpu.VMEM((plan.width, full, c), bf16),
        pltpu.VMEM((cells, c), bf16),
        pltpu.VMEM((cells, c), f32),
        pltpu.VMEM(plan.wide(plan.width), f32),
        pltpu.VMEM(plan.wide(plan.padded), f32),
    ]
    return call(
        functools.partial(step_kernel, plan, len(received)),
        "backward",
        [og, *received, scale, gain, w_in, w_out, gate, mask, standard, inv, taps],
        outs,
        scratch,
        4 * cells * c * plan.hidden,
    )


def turn_kernel(hidden_ref, normed_ref, hidden_t_ref, normed_t_ref):
    hidden_t_ref[...] = hidden_ref[...].astype(f32).T.astype(bf16)
    normed_t_ref[...] = normed_ref[...].astype(f32).T.astype(bf16)


def turn(hidden, normed):
    outs = [shape(hidden.shape[::-1], bf16), shape(normed.shape[::-1], bf16)]
    return call(turn_kernel, "turn", [hidden, normed], outs, [], 1000)


def out_share(plan):
    return plan.hidden // plan.cols


def in_share(plan):
    rows = plan.channels // plan.cols
    return rows, plan.hidden // plan.part * rows


def taps_rows(plan):
    return -(-(plan.side**2) // 16) * 16


def put(halves_ref, bit, share, row, value):
    half = bit if share % 2 == 0 else 1 - bit
    halves_ref[half, share // 2, pl.ds(row, value.shape[0]), :] = value


def out_kernel(plan, n_received, og_ref, *refs):
    received = refs[:n_received] or None
    scale_ref, mask_ref, hidden_t_ref, g_ref, bg_ref, halves_ref, send_ref, edge_ref = refs[n_received:]
    load_upstream(plan, g_ref, og_ref, received, edge_ref)
    branch(plan, g_ref, scale_ref, mask_ref, bg_ref)
    bit = lax.rem(lax.axis_index("col"), 2)
    rows = out_share(plan)
    piece = min(plan.part, rows)
    for n in range(plan.hidden // plan.part):
        at = pl.ds(n * plan.part, plan.part)
        grad_out = jnp.dot(hidden_t_ref[at, :], bg_ref[...], preferred_element_type=f32)
        for start in range(0, plan.part, piece):
            unit = n * plan.part + start
            put(halves_ref, bit, unit // rows, unit % rows, grad_out[start : start + piece])
    for u in range(plan.cols // 2):
        send_ref[pl.ds(u * rows, rows), :] = halves_ref[1, u].astype(bf16)


def out_step(plan, og, received, scale, mask, hidden_t):
    c, full, cells, half = plan.channels, plan.full, plan.cells, plan.cols // 2
    rows = out_share(plan)
    outs = [
        shape((plan.width, full, c), bf16),
        shape((cells, c), bf16),
        shape((2, half, rows, c), f32),
        shape((half * rows, c), bf16),
    ]
    return call(
        functools.partial(out_kernel, plan, len(received)),
        "grad_out",
        [og, *received, scale, mask, hidden_t],
        outs,
        [pltpu.VMEM(plan.wide(plan.padded), f32)],
        2 * cells * c * plan.hidden,
    )


def in_kernel(plan, bg_ref, w_in_ref, w_out_ref, gate_ref, normed_t_ref, ng_ref, halves_ref):
    bit = lax.rem(lax.axis_index("col"), 2)
    rows, _ = in_share(plan)
    for n in range(plan.hidden // plan.part):
        at = pl.ds(n * plan.part, plan.part)
        hidden_grad = contract_last(bg_ref[...], w_out_ref[at, :])
        pre_grad = (hidden_grad * gate_ref[:, at].astype(f32)).astype(bf16)
        term = contract_last(pre_grad, w_in_ref[:, at])
        ng_ref[...] = term if n == 0 else ng_ref[...] + term
        grad_in = jnp.dot(normed_t_ref[...], pre_grad, preferred_element_type=f32)
        for share in range(plan.cols):
            put(halves_ref, bit, share, n * rows, grad_in[share * rows : (share + 1) * rows])


def in_step(plan, bg, w_in, w_out, gate, normed_t):
    c, cells = plan.channels, plan.cells
    outs = [shape((cells, c), f32), shape((2, plan.cols // 2, in_share(plan)[1], c), f32)]
    return call(
        functools.partial(in_kernel, plan),
        "grad_in",
        [bg, w_in, w_out, gate, normed_t],
        outs,
        [],
        6 * cells * c * plan.hidden,
    )


def taps_kernel(plan, ng_ref, halves_ref, gain_ref, standard_ref, inv_ref, xw_ref, cg_ref, send_ref, *edges):
    full, width, side = plan.full, plan.width, plan.side
    _, share_rows = in_share(plan)
    norm_back(plan, ng_ref, gain_ref, standard_ref, inv_ref, cg_ref)
    put_edges(plan, cg_ref, edges)
    count = plan.cols // 2
    for u in range(count):
        send_ref[pl.ds(u * share_rows, share_rows), :] = halves_ref[1, u].astype(bf16)
    rows = []
    for i in range(side):
        pieces = [[] for _ in range(side)]
        for half in range(plan.halves):
            totals = [jnp.zeros((8, LANES), f32) for _ in range(side)]
            for block in range(full // 8):
                window = xw_ref[half, :, pl.ds(PAD - plan.margin + i + 8 * block, 8), :]
                grad = cg_ref[half, :, pl.ds(PAD + 8 * block, 8), :]
                for j in range(side):
                    totals[j] = totals[j] + jnp.sum(window[j : j + width] * grad, axis=0)
            for j in range(side):
                pieces[j].append(jnp.sum(totals[j], axis=0, keepdims=True))
        rows += [jnp.concatenate(p, axis=-1) for p in pieces]
    rows.append(jnp.zeros((taps_rows(plan) - side**2, plan.channels), f32))
    at = pl.ds(count * share_rows, taps_rows(plan))
    send_ref[at, :] = jnp.concatenate(rows, axis=0).astype(bf16)


def taps_step(plan, norm_grad, halves, gain, standard, inv, xw):
    c, full = plan.channels, plan.full
    outs = [
        shape(plan.wide(plan.width), f32),
        shape((plan.cols // 2 * in_share(plan)[1] + taps_rows(plan), c), bf16),
        *edge_shapes(plan),
    ]
    return call(
        functools.partial(taps_kernel, plan),
        "grad_taps",
        [norm_grad, halves, gain, standard, inv, xw],
        outs,
        [],
        2 * plan.cells * c * plan.side**2,
    )


def finish_kernel(plan, g_ref, cg_ref, taps_ref, *refs):
    edges, (new_ref, edge_ref) = refs[:-2], refs[-2:]
    fill_edges(plan, edge_ref, edges)
    for half, block in blocks(plan):
        if block % 2:
            continue
        lanes = pl.ds(half * LANES, LANES)
        own = [own_sums(plan, cg_ref, taps_ref, half, block + k) for k in range(2)]
        rest = [edge_sums(plan, edge_ref, taps_ref, half, block + k) for k in range(2)]
        r, at = divmod(8 * block, plan.height)
        for q in range(plan.width):
            moved = jnp.concatenate([own[k][q] + rest[k][q] for k in range(2)], axis=0)
            upstream = g_ref[q, pl.ds(8 * block, 16), lanes].astype(f32)
            new_ref[r, q, pl.ds(at, 16), lanes] = (upstream + moved).astype(bf16)


def finish(plan, upstream, conv_grad, taps, edges):
    c = plan.channels
    return call(
        functools.partial(finish_kernel, plan),
        "finish",
        [upstream, conv_grad, taps, *edges],
        [shape((plan.rows, plan.width, plan.height, c), bf16)],
        [pltpu.VMEM(plan.wide(plan.padded), f32)],
        2 * plan.cells * c * plan.side**2,
    )[0]


def swap(value, axis, bit):
    size = lax.axis_size(axis)
    return lax.ppermute(value, axis, [(i, i ^ bit) for i in range(size)])


def combine_kernel(bit, share_rows, extra, keep_ref, sent_ref, got_ref, send_ref, next_ref):
    count = keep_ref.shape[1]
    mine = lax.rem(lax.axis_index("col") // bit, 2)
    for u in range(count // 2):
        for half in range(2):
            share = 2 * u + (mine if half == 0 else 1 - mine)
            at = pl.ds(pl.multiple_of(share * share_rows, 16), share_rows)
            value = keep_ref[0, share] + got_ref[at, :].astype(f32)
            if half == 0:
                next_ref[0, u] = value
            else:
                send_ref[pl.ds(u * share_rows, share_rows), :] = value.astype(bf16)
    if extra:
        old = pl.ds(count * share_rows, extra)
        new = pl.ds(count // 2 * share_rows, extra)
        send_ref[new, :] = (sent_ref[old, :].astype(f32) + got_ref[old, :].astype(f32)).astype(bf16)


def close_kernel(share_rows, extra, keep_ref, sent_ref, got_ref, out_ref):
    at = pl.ds(0, share_rows)
    out_ref[at, :] = (keep_ref[0, 0] + got_ref[at, :].astype(f32)).astype(bf16)
    if extra:
        rest = pl.ds(share_rows, extra)
        out_ref[rest, :] = (sent_ref[rest, :].astype(f32) + got_ref[rest, :].astype(f32)).astype(bf16)


class Reduction:
    def __init__(self, plan, halves, send, share_rows, extra):
        self.plan, self.share_rows, self.extra = plan, share_rows, extra
        self.keep, self.send, self.bit = halves, send, 1
        self.total = None
        if plan.cols > 2:
            self.next_stage()

    def next_stage(self):
        c = self.plan.channels
        got = swap(self.send, "col", self.bit)
        self.bit *= 2
        count = self.keep.shape[1] // 2
        self.send, self.keep = call(
            functools.partial(combine_kernel, self.bit, self.share_rows, self.extra),
            "combine",
            [self.keep, self.send, got],
            [
                shape((count * self.share_rows + self.extra, c), bf16),
                shape((1, count, self.share_rows, c), f32),
            ],
            [],
            1000,
        )

    def close(self, after=None):
        plan = self.plan
        while 2 * self.bit < plan.cols:
            self.next_stage()
        got = swap(self.send, "col", self.bit)
        if after is not None:
            got, _ = lax.optimization_barrier((got, after))
        self.total = call(
            functools.partial(close_kernel, self.share_rows, self.extra),
            "close",
            [self.keep, self.send, got],
            [shape((self.share_rows + self.extra, plan.channels), bf16)],
            [],
        )[0]

    def terms(self):
        plan, total = self.plan, self.total
        terms = [total]
        bit = 1
        while bit < plan.rows:
            terms = [total, swap(total, "row", bit)]
            bit *= 2
            if bit < plan.rows:
                total = (terms[0].astype(f32) + terms[1].astype(f32)).astype(bf16)
        return terms


def read(refs, scale, start, count):
    return scale * sum(ref[pl.ds(start, count), :].astype(f32) for ref in refs)


def out_result_kernel(plan, scale, *refs):
    refs[-1][...] = read(refs[:-1], scale, 0, out_share(plan))


def in_result_kernel(plan, scale, *refs):
    terms, (in_ref, taps_ref) = refs[:-2], refs[-2:]
    rows, share_rows = in_share(plan)
    for n in range(plan.hidden // plan.part):
        in_ref[:, pl.ds(n * plan.part, plan.part)] = read(terms, scale, n * rows, rows)
    sums = read(terms, scale, share_rows, taps_rows(plan))
    for i in range(plan.side):
        for j in range(plan.side):
            row = i * plan.side + j
            taps_ref[i, j] = sums[row : row + 1]


def out_result(plan, scale, terms):
    kernel = functools.partial(out_result_kernel, plan, scale)
    return call(kernel, "out_result", terms, [shape((out_share(plan), plan.channels), f32)], [], 1000)[0]


def in_result(plan, scale, terms):
    outs = [
        shape((in_share(plan)[0], plan.hidden), f32),
        shape((plan.side, plan.side, 1, plan.channels), f32),
    ]
    return call(functools.partial(in_result_kernel, plan, scale), "in_result", terms, outs, [], 1000)


def to_tile(plan, strips):
    rows, cols = plan.rows, plan.cols
    me = lax.axis_index("row")
    tile = jnp.zeros((rows, *strips.shape[1:]), strips.dtype)
    own = lax.dynamic_index_in_dim(strips, me, 0, keepdims=True)
    tile = lax.dynamic_update_slice_in_dim(tile, own, plan.place(me), 0)
    for dr in range(1, rows):
        target = lax.rem(me + dr, rows)
        piece = lax.dynamic_index_in_dim(strips, target, 0, keepdims=True)
        got = lax.ppermute(piece, "row", [(r, (r + dr) % rows) for r in range(rows)])
        source = plan.place(lax.rem(me - dr + rows, rows))
        tile = lax.dynamic_update_slice_in_dim(tile, got, source, 0)
    tile = tile.reshape(plan.across, plan.height, plan.channels)
    return jnp.swapaxes(tile, 0, 1)


def one_crop(plan, norm_scale, tissue, saved, out_grad, params):
    mains = exchange_mains(plan, pack(plan, saved))
    pieces = [*mains, *exchange_sides(plan, pack_sides(plan, mains))]
    upstream = exchange_mains(plan, pack_upstream(plan, tissue, out_grad))
    taps_above = to_segment_below(plan, params[0])
    taps, w_in, w_out, conv_bias, gain, bias, b_in, scale = load(params)
    xw, standard, inv, gate, hidden, normed = forward(
        plan, pieces, taps, conv_bias, gain, bias, w_in, b_in
    )
    og, mask, taps_above = lax.optimization_barrier((*upstream_strip(plan, upstream), taps_above))
    step_params, kept = (scale, gain, w_in, w_out, taps), (standard, inv, gate, mask)
    received, turned = [], None
    for _ in range(plan.segments - 1):
        own, *edges = backward_step(plan, og, received, step_params, kept)
        received = [taps_above, to_segment_below(plan, own), *send_edges(plan, edges, -1)]
        if turned is None:
            hidden, normed, _ = lax.optimization_barrier((hidden, normed, own))
            turned = turn(hidden, normed)
    hidden_t, normed_t = turned if turned is not None else turn(hidden, normed)
    upstream, branch_grad, halves, send = out_step(plan, og, received, scale, mask, hidden_t)
    out_sum = Reduction(plan, halves, send, out_share(plan), 0)
    norm_grad, halves = in_step(plan, branch_grad, w_in, w_out, gate, normed_t)
    norm_grad, _ = lax.optimization_barrier((norm_grad, out_sum.send))
    conv_grad, send, *edges = taps_step(plan, norm_grad, halves, gain, standard, inv, xw)
    in_sum = Reduction(plan, halves, send, in_share(plan)[1], taps_rows(plan))
    out_sum.close()
    grad_out = out_result(plan, norm_scale, out_sum.terms())
    edges, _ = lax.optimization_barrier((edges, in_sum.send))
    strips = finish(plan, upstream, conv_grad, taps, send_edges(plan, edges, 0))
    in_sum.close()
    grad_in, grad_taps = in_result(plan, norm_scale, in_sum.terms())
    return to_tile(plan, strips), grad_in, grad_out, grad_taps


def per_device(
    saved_inputs,
    out_grad,
    tissue,
    conv_taps,
    conv_bias,
    norm_gain,
    norm_bias,
    w_in,
    b_in,
    w_out,
    layer_scale,
):
    crop_count, height, across, channels = out_grad.shape
    plan = Plan(
        lax.axis_size("segment"),
        lax.axis_size("row"),
        lax.axis_size("col"),
        height,
        across,
        channels,
        w_in.shape[2],
        conv_taps.shape[1],
    )
    norm_scale = 1.0 / math.sqrt(crop_count * plan.full * across * plan.cols)
    params = (conv_taps.transpose(1, 2, 0, 3), w_in[0], w_out[0], conv_bias, norm_gain, norm_bias, b_in, layer_scale)
    results = [
        one_crop(plan, norm_scale, tissue[crop], saved_inputs[0, crop], out_grad[crop], params)
        for crop in range(crop_count)
    ]
    grads, *weights = zip(*results)
    grad_in, grad_out, grad_taps = (sum(w[1:], w[0]) for w in weights)
    return (jnp.stack(grads)[None], grad_in[None], grad_out[None], grad_taps.transpose(2, 0, 1, 3))


def solution(mesh):
    return jax.shard_map(
        per_device,
        mesh=mesh,
        in_specs=(
            P("segment", None, "row", "col", None),
            P(None, "row", "col", None),
            P(None, "row", "col"),
            P("segment", None, None, None),
            P("segment", None),
            P("segment", None),
            P("segment", None),
            P("segment", None, None),
            P("segment", None),
            P("segment", None, None),
            P("segment", None),
        ),
        out_specs=(
            P("segment", None, "row", "col", None),
            P("segment", "col", None),
            P("segment", "col", None),
            P("segment", None, None, None),
        ),
        check_vma=False,
    )
```
